32 devices in a mesh: groups: 2 (over y), tile: 4 (over z), sect: 2 (over x), half: 2 (over core).
Axes of the slice: x: 2, y: 2, z: 4, core: 2. Of those that a mesh axis runs over, the one named last changes fastest.
Arguments:
- patches: bfloat16 [4, 4, 32, 256, 256], P(('groups', 'sect'), 'tile', 'half'), parts along dimension 0, may hold values from -6 to 6
- pair_lists: int32 [3, 4, 4, 24], P(None, ('groups', 'sect'), 'tile', 'half'), parts along dimension 1, may hold values from 0 to 15, as said below
- move_plan: int32 [2, 4, 4, 24], P(None, ('groups', 'sect'), 'tile', 'half'), parts along dimension 1, may hold values from -1 to 5, as said below
Outputs:
- work_surfaces: float32 [4, 4, 12, 256, 256], P(('groups', 'sect'), 'tile', 'half'), parts along dimension 0
- peak_values: float32 [4, 4, 24], P(('groups', 'sect'), 'tile', 'half'), parts along dimension 0
The draws below stay inside these ranges and needn't reach their ends.
There are 2 independent parts, one for each index of `groups`. The reference program is written for one: setup_inputs(seed, part) draws one part's arguments, and reference() takes and returns one part's arrays. A program takes and returns all parts, laid end to end along the dimension named above; each array names one. Nothing has to cross between parts.
Inputs may be any that keep to these rules, and one draw needn't show every extreme that they name: `pair_lists`: kind 0 names the tile row below (r + 1), kind 1 the next section (s + 1). Every slot of the last tile row has kind 1 and every slot of the last section kind 0; the device of the last tile row in the last section has no live slot. Entries a and b are below 16. `move_plan`: entry 0 is the target tile row of a slot (-1 for unused), entry 1 its work slot there (-1 for unused). A device has at most 12 live slots and at most 3 live slots with the same target; within one section and column half no two live slots share a target and a work slot, work slots are below 6, and live slots are all assigned. Some device has 12 live slots and some target receives 6.
All inputs are finite; a program needn't handle non-finite values.
Results may differ from the reference program's by a relative error of at most 0.0003.
Values may be sent and summed in bfloat16 or wider, within the bound.
No kernel may reach another device: no remote copies, remote signals or barrier semaphores. Data moves between devices by JAX's collectives and lax.ppermute only.
A program may use at most 64 MiB of HBM per device.

```python
import jax
import jax.numpy as jnp
from jax import lax

PS = 256
PATCHES = 16
SLOTS = 12
WORK = 6
TILE_ROWS = 4
SECTIONS = 2


def draw_pair_lists(key, part):
    subkeys = jax.random.split(jax.random.fold_in(key, 11), 3)
    grid_shape = (SECTIONS, TILE_ROWS, 2 * SLOTS)
    pair_kinds = jax.random.randint(subkeys[0], grid_shape, 0, 2)
    sect_ids = jnp.arange(SECTIONS, dtype=jnp.int32)[:, None, None]
    row_ids = jnp.arange(TILE_ROWS, dtype=jnp.int32)[None, :, None]
    pair_kinds = jnp.where(row_ids == TILE_ROWS - 1, 1, pair_kinds)
    pair_kinds = jnp.where(sect_ids == SECTIONS - 1, 0, pair_kinds)
    first_index = jax.random.randint(subkeys[1], grid_shape, 0, PATCHES)
    second_index = jax.random.randint(subkeys[2], grid_shape, 0, PATCHES)
    return jnp.stack([pair_kinds, first_index, second_index]).astype(jnp.int32)


def draw_move_plan(key, part):
    subkeys = jax.random.split(jax.random.fold_in(key, 23), 7)
    columns = SECTIONS * 2
    rows_total = TILE_ROWS
    row_ids = jnp.arange(rows_total, dtype=jnp.int32)
    heavy_row = jax.random.randint(subkeys[0], (columns,), 0, rows_total - 1)
    totals = jax.random.randint(subkeys[1], (columns,), rows_total * (WORK - 1) + 1, rows_total * WORK + 1)
    weights = jax.random.randint(subkeys[2], (columns, rows_total), 1, 4)
    sect_of = jnp.arange(columns, dtype=jnp.int32) // 2
    blocked = (sect_of[:, None] == SECTIONS - 1) & (row_ids[None, :] == rows_total - 1)
    is_heavy = row_ids[None, :] == heavy_row[:, None]
    weights = jnp.where(blocked | is_heavy, 0, weights)
    weight_sum = jnp.maximum(jnp.sum(weights, axis=1, keepdims=True), 1)
    shares = jnp.minimum((totals[:, None] - SLOTS) * weights // weight_sum, SLOTS)
    counts = jnp.where(is_heavy, SLOTS, shares).astype(jnp.int32)
    visit_scores = jax.random.randint(subkeys[3], (columns, rows_total), 0, 1 << 20) * rows_total + row_ids[None, :]
    visits = jnp.argsort(visit_scores, axis=1).astype(jnp.int32)

    def fill_step(step, carried):
        counts_now, leftover = carried
        device_row = visits[:, step]
        onehot = row_ids[None, :] == device_row[:, None]
        spare_room = jnp.sum(jnp.where(onehot & ~blocked, SLOTS - counts_now, 0), axis=1)
        added = jnp.minimum(spare_room, leftover)
        return (counts_now + jnp.where(onehot, added[:, None], 0), leftover - added)
    leftover = totals - jnp.sum(counts, axis=1)
    counts, leftover = lax.fori_loop(0, rows_total, fill_step, (counts, leftover))
    slot_ids = jnp.arange(SLOTS, dtype=jnp.int32)
    scores = jax.random.randint(subkeys[4], (columns, rows_total, SLOTS), 0, 1 << 20) * SLOTS + slot_ids
    ranks = jnp.argsort(jnp.argsort(scores, axis=2), axis=2)
    is_live = ranks < counts[:, :, None]
    before = jnp.cumsum(is_live.astype(jnp.int32), axis=2) - 1
    order_scores = jax.random.randint(subkeys[5], (columns, rows_total), 0, 1 << 20) * rows_total + row_ids[None, :]
    positions = jnp.argsort(jnp.argsort(order_scores, axis=1), axis=1)
    earlier = positions[:, None, :] < positions[:, :, None]
    offset = jnp.sum(jnp.where(earlier, counts[:, None, :], 0), axis=2)
    global_rank = offset[:, :, None] + before
    dest_scores = jax.random.randint(subkeys[6], (columns, rows_total), 0, 1 << 20) * rows_total + row_ids[None, :]
    dest_perm = jnp.argsort(dest_scores, axis=1).astype(jnp.int32)
    residue = (global_rank % rows_total).reshape(columns, rows_total * SLOTS)
    destination = jnp.take_along_axis(dest_perm, residue, axis=1).reshape(columns, rows_total, SLOTS)
    targets = jnp.where(is_live, destination, -1)
    places = jnp.where(is_live, global_rank // rows_total, -1)

    def arrange(values):
        shaped = values.reshape(SECTIONS, 2, rows_total, SLOTS).transpose(0, 2, 1, 3)
        return shaped.reshape(SECTIONS, rows_total, 2 * SLOTS)
    return jnp.stack([arrange(targets), arrange(places)]).astype(jnp.int32)


def block_levels(rng, extent, pieces, smallest, high):
    factor_of, own = 1.0, jax.random.fold_in(rng, 6)
    for position, shards_of in pieces:
        steps = jnp.exp(jax.random.uniform(jax.random.fold_in(own, position), (shards_of,), jnp.float32, smallest / len(pieces), high / len(pieces)))
        factor_of = factor_of * jnp.repeat(steps, extent[position] // shards_of).reshape([-1 if axis == position else 1 for axis in range(len(extent))])
    return factor_of


def gaussian(stream_key, extent, spread, bound, cuts=(), kind=jnp.bfloat16):
    drawn = jax.random.normal(stream_key, extent, jnp.float32) * spread
    if len(cuts) > 0:
        drawn = block_levels(stream_key, extent, cuts, -0.22, 0.18) * drawn
    return jnp.clip(drawn, min=-bound, max=bound).astype(kind)


def setup_inputs(seed: int = 0, part: int = 0) -> dict:
    arg_keys = jax.random.split(jax.random.key(seed), 4)
    part_keys = jax.random.split(jax.random.fold_in(arg_keys[3], part), 4)
    return {
        "patches": gaussian(part_keys[0], (SECTIONS, TILE_ROWS, 2 * PATCHES, PS, PS), 1.0, 6.0, ((0, 2), (1, 4), (2, 2))),
        "pair_lists": draw_pair_lists(jax.random.fold_in(jax.random.fold_in(arg_keys[3], part), 71), part),
        "move_plan": draw_move_plan(jax.random.fold_in(jax.random.fold_in(arg_keys[3], part), 71), part),
    }


FLOOR = 0.05


def surface_of(first_patch, second_patch):
    spec_first = jnp.fft.fft2(first_patch.astype(jnp.float32))
    spec_second = jnp.fft.fft2(second_patch.astype(jnp.float32))
    cross_power = spec_first * jnp.conj(spec_second)
    scaled = cross_power / jnp.maximum(jnp.abs(cross_power), FLOOR * PS * PS)
    return (jnp.real(jnp.fft.ifft2(scaled)) * PS).astype(jnp.float32)


def reference(patches, pair_lists, move_plan):
    halves = 2
    flat_patches = patches.reshape(SECTIONS * TILE_ROWS * halves * PATCHES, PS, PS)
    grid = (SECTIONS, TILE_ROWS, halves, SLOTS)
    sect_ids = jnp.arange(SECTIONS, dtype=jnp.int32)[:, None, None, None]
    row_ids = jnp.arange(TILE_ROWS, dtype=jnp.int32)[None, :, None, None]
    half_ids = jnp.arange(halves, dtype=jnp.int32)[None, None, :, None]
    slot_ids = jnp.arange(SLOTS, dtype=jnp.int32)[None, None, None, :]
    pair_kinds = pair_lists[0].reshape(grid)
    first_index = pair_lists[1].reshape(grid)
    second_index = pair_lists[2].reshape(grid)
    targets = move_plan[0].reshape(grid)
    places = move_plan[1].reshape(grid)
    slot_alive = targets >= 0
    patch_total = SECTIONS * TILE_ROWS * halves * PATCHES
    first_flat = ((sect_ids * TILE_ROWS + row_ids) * halves + half_ids) * PATCHES + first_index
    partner_sect = sect_ids + pair_kinds
    partner_row = row_ids + 1 - pair_kinds
    second_flat = ((partner_sect * TILE_ROWS + partner_row) * halves + half_ids) * PATCHES + second_index
    first_flat = jnp.clip(first_flat, 0, patch_total - 1).astype(jnp.int32)
    second_flat = jnp.clip(second_flat, 0, patch_total - 1).astype(jnp.int32)
    work_total = SECTIONS * TILE_ROWS * halves * WORK
    work_flat = ((sect_ids * TILE_ROWS + targets) * halves + half_ids) * WORK + places
    work_flat = jnp.where(slot_alive, work_flat, work_total).astype(jnp.int32)
    slot_flat = (((sect_ids * TILE_ROWS + row_ids) * halves + half_ids) * SLOTS + slot_ids) + jnp.zeros(grid, jnp.int32)
    source = jnp.full((work_total + 1,), -1, jnp.int32).at[work_flat.reshape(-1)].set(slot_flat.reshape(-1).astype(jnp.int32))[:work_total]
    is_valid = source >= 0
    safe_source = jnp.maximum(source, 0)
    first_pick = first_flat.reshape(-1)[safe_source]
    second_pick = second_flat.reshape(-1)[safe_source]

    def one_entry(entry):
        pick_first, pick_second, valid_entry = entry
        surface = surface_of(flat_patches[pick_first], flat_patches[pick_second])
        return jnp.where(valid_entry, surface, jnp.zeros_like(surface))

    surfaces = lax.map(one_entry, (first_pick, second_pick, is_valid))
    work_peaks = jnp.max(surfaces, axis=(1, 2))
    slot_peaks = work_peaks[jnp.clip(work_flat, 0, work_total - 1).reshape(-1)].reshape(grid)
    peak_values = jnp.where(slot_alive, slot_peaks, jnp.zeros_like(slot_peaks))
    work_surfaces = surfaces.reshape(SECTIONS, TILE_ROWS, halves * WORK, PS, PS)
    return work_surfaces, peak_values.reshape(SECTIONS, TILE_ROWS, halves * SLOTS)
```

```python
import functools

import jax
import jax.numpy as jnp
import ml_dtypes
import numpy as np
from jax import lax
from jax.experimental import pallas as pl
from jax.experimental.pallas import tpu as pltpu
from jax.sharding import PartitionSpec as P

FLOOR = 0.05
TOP = 32767.0
TINY = 1e-28
LIMIT = 48 * 1024 * 1024

SMEM = pl.BlockSpec(memory_space=pltpu.SMEM)
VMEM = pl.BlockSpec(memory_space=pltpu.VMEM)
ANY = pl.BlockSpec(memory_space=pl.ANY)
SDS = jax.ShapeDtypeStruct


def shifted(value, axis, steps):
    count = lax.axis_size(axis)
    pairs = [(i, i + steps) for i in range(count) if 0 <= i + steps < count]
    return lax.ppermute(value, axis, pairs)


def rotated(value, axis, steps):
    count = lax.axis_size(axis)
    return lax.ppermute(value, axis, [(i, (i + steps) % count) for i in range(count)])


def packed_table(length):
    half = length // 2
    n = np.arange(length)[:, None]
    v = np.arange(half + 1)[None, :]
    angle = 2.0 * np.pi * ((n * v) % length) / length
    table = np.concatenate([np.cos(angle), np.sin(angle[:, 1:half])], axis=1)
    high = table.astype(np.float32).astype(ml_dtypes.bfloat16)
    low = (table - high.astype(np.float64)).astype(np.float32).astype(ml_dtypes.bfloat16)
    return high, low


def dot(left, right):
    return jnp.dot(left, right, preferred_element_type=jnp.float32)


def pieces(value):
    high = value.astype(jnp.bfloat16)
    low = (value - high.astype(jnp.float32)).astype(jnp.bfloat16)
    return high, low


def packed_transform(picture, th, tl, sh, sl):
    high, low = pieces(dot(picture, th[...]) + dot(picture, tl[...]))
    return dot(sh[...], high) + dot(sh[...], low) + dot(sl[...], high)


def two_lines(packed, half, row, col, edge):
    cp, cq = packed[:half, :half], packed[:half, half:]
    sp, sq = packed[half:, :half], packed[half:, half:]
    sq_in = jnp.where(edge, 0.0, sq)
    re1 = cp - sq_in
    im1 = -(jnp.where(row, 0.0, sp) + jnp.where(col, 0.0, cq))
    re2 = jnp.where(row, sp, jnp.where(col, cq, cp + sq))
    im2 = jnp.where(edge, -sq, sp - cq)
    return re1, im1, re2, im2


def normalized_packed(one, two, length):
    half = length // 2
    floor = FLOOR * length * length
    rows = lax.broadcasted_iota(jnp.int32, (half, half), 0)
    cols = lax.broadcasted_iota(jnp.int32, (half, half), 1)
    row, col = rows == 0, cols == 0
    edge, corner = row | col, row & col
    a_re1, a_im1, a_re2, a_im2 = two_lines(one, half, row, col, edge)
    b_re1, b_im1, b_re2, b_im2 = two_lines(two, half, row, col, edge)

    def scaled(a_re, a_im, b_re, b_im):
        re = a_re * b_re + a_im * b_im
        im = a_im * b_re - a_re * b_im
        factor = jnp.minimum(lax.rsqrt(re * re + im * im), 1.0 / floor)
        return re * factor, im * factor

    n_re1, n_im1 = scaled(a_re1, a_im1, b_re1, b_im1)
    n_re2, n_im2 = scaled(a_re2, a_im2, b_re2, b_im2)

    def real_corner(value, start_row, start_col):
        a = one[start_row : start_row + half, start_col : start_col + half]
        b = two[start_row : start_row + half, start_col : start_col + half]
        product = a * b
        alone = 0.5 * product / jnp.maximum(jnp.abs(product), floor)
        return jnp.where(corner, alone, value)

    cp = jnp.where(edge, n_re1, n_re1 + n_re2)
    cq = jnp.where(row, -n_im1, jnp.where(col, n_re2, -(n_im1 + n_im2)))
    sp = jnp.where(row, n_re2, jnp.where(col, -n_im1, n_im2 - n_im1))
    sq = jnp.where(edge, -n_im2, n_re2 - n_re1)
    cp = real_corner(cp, 0, 0)
    cq = real_corner(cq, 0, half)
    sp = real_corner(sp, half, 0)
    sq = real_corner(sq, half, half)
    packed = jnp.concatenate(
        [jnp.concatenate([cp, cq], axis=1), jnp.concatenate([sp, sq], axis=1)], axis=0
    )
    return packed * (2.0 / length)


def inverse_packed(packed, th, tl, sh, sl):
    high, low = pieces(packed)
    high, low = pieces(dot(th[...], high) + dot(th[...], low) + dot(tl[...], high))
    return dot(high, sh[...]) + dot(high, sl[...]) + dot(low, sh[...])


def lanes_kernel(tiles, per, info, table):
    slots = info.shape[1]
    me = lax.axis_index("tile")
    for d in range(tiles):
        for j in range(per):
            table[0, d * per + j] = -1
            for field in range(1, 4):
                table[field, d * per + j] = 0
            table[4, d * per + j] = -1
    for k in range(slots):
        target = info[3, k]
        rank = jnp.int32(0)
        for q in range(k):
            rank += (info[3, q] == target).astype(jnp.int32)
        distance = lax.rem(target - me + tiles, tiles)
        lane = distance * per + rank

        @pl.when(target >= 0)
        def _():
            table[0, lane] = info[0, k]
            table[1, lane] = info[1, k]
            table[2, lane] = info[2, k]
            table[3, lane] = info[4, k]
            table[4, lane] = k


def gather_kernel(first_lane, per, below, later, patches, to_below, to_later, sems):
    copies = []
    for j in range(per):
        lane = first_lane + j
        copies.append(
            pltpu.make_async_copy(patches.at[below[2, lane]], to_below.at[j], sems.at[0, j])
        )
        copies.append(
            pltpu.make_async_copy(patches.at[later[2, lane]], to_later.at[j], sems.at[1, j])
        )
    for copy in copies:
        copy.start()
    for copy in copies:
        copy.wait()


def pair_kernel(first_lane, table, own, below, later, th, tl, sh, sl, codes, tags):
    j = pl.program_id(0)
    lane = first_lane + j
    kind = table[0, lane]
    length = own.shape[-1]
    tags[j, 0] = 0.0
    tags[j, 1] = -1.0
    tags[j, 2] = 0.0

    @pl.when(kind >= 0)
    def _():
        second = jnp.where(kind == 0, below[0], later[0])
        one = packed_transform(own[0], th, tl, sh, sl)
        two = packed_transform(second, th, tl, sh, sl)
        surface = inverse_packed(normalized_packed(one, two, length), th, tl, sh, sl)
        peak = jnp.max(surface)
        size = jnp.maximum(jnp.maximum(peak, -jnp.min(surface)), TINY)
        grown = jnp.abs(surface) * (TOP * TOP / size)
        root = grown * lax.rsqrt(jnp.maximum(grown, TINY))
        whole = (root + 0.5).astype(jnp.int32)
        codes[0] = jnp.where(surface < 0, -whole, whole).astype(jnp.int16)
        tags[j, 0] = size
        tags[j, 1] = table[3, lane].astype(jnp.float32)
        tags[j, 2] = peak


def settle_kernel(shifts, per, table, *refs):
    count = len(shifts)
    home_tags = refs[:count]
    tags = refs[count : 2 * count]
    codes = refs[2 * count : 3 * count]
    surfaces, peaks = refs[3 * count :]
    surfaces[...] = jnp.zeros_like(surfaces)
    for k in range(peaks.shape[0]):
        peaks[k] = 0.0
    for i, d in enumerate(shifts):
        for j in range(per):
            slot = table[4, d * per + j]

            @pl.when(slot >= 0)
            def _():
                peaks[slot] = home_tags[i][j, 2]

            place = tags[i][j, 1].astype(jnp.int32)

            @pl.when(place >= 0)
            def _():
                value = codes[i][j].astype(jnp.int32).astype(jnp.float32)
                surfaces[place] = value * jnp.abs(value) * (tags[i][j, 0] / (TOP * TOP))


def params():
    return pltpu.CompilerParams(vmem_limit_bytes=LIMIT)


def body(patches, pair_lists, move_plan):
    own = patches[0, 0]
    count, length, _ = own.shape
    info = jnp.concatenate([pair_lists[:, 0, 0], move_plan[:, 0, 0]], axis=0)
    slots = info.shape[1]
    tiles = lax.axis_size("tile")
    per = (slots + tiles - 1) // tiles
    lanes = tiles * per
    shifts = sorted(range(tiles), key=lambda d: (d == 0, -min(d, tiles - d), d))

    table = pl.pallas_call(
        functools.partial(lanes_kernel, tiles, per),
        out_shape=SDS((5, lanes), jnp.int32),
        in_specs=[SMEM],
        out_specs=SMEM,
        name="lanes",
    )(info)
    table_above = shifted(table, "tile", 1)
    table_before = shifted(table, "sect", 1)

    high, low = packed_table(length)
    tables = [jnp.asarray(t) for t in (high, low, high.T.copy(), low.T.copy())]
    picture = SDS((per, length, length), jnp.bfloat16)

    arrivals = []
    for d in shifts:
        to_below, to_later = pl.pallas_call(
            functools.partial(gather_kernel, d * per, per),
            out_shape=(picture, picture),
            in_specs=[SMEM, SMEM, ANY],
            out_specs=(ANY, ANY),
            scratch_shapes=[pltpu.SemaphoreType.DMA((2, per))],
            name=f"gather_{d}",
        )(table_above, table_before, own)
        arrivals.append((shifted(to_below, "tile", -1), shifted(to_later, "sect", -1)))

    square = (1, length, length)
    whole = pl.BlockSpec((length, length), lambda j, t: (0, 0))
    home_tags, tags, codes = [], [], []
    for d, (below, later) in zip(shifts, arrivals):
        lane_codes, lane_tags = pl.pallas_call(
            functools.partial(pair_kernel, d * per),
            out_shape=(
                SDS((per, length, length), jnp.int16),
                SDS((per, 3), jnp.float32),
            ),
            grid_spec=pltpu.PrefetchScalarGridSpec(
                num_scalar_prefetch=1,
                grid=(per,),
                in_specs=[
                    pl.BlockSpec(square, lambda j, t, d=d: (t[1, d * per + j], 0, 0)),
                    pl.BlockSpec(square, lambda j, t: (j, 0, 0)),
                    pl.BlockSpec(square, lambda j, t: (j, 0, 0)),
                ]
                + [whole] * 4,
                out_specs=(pl.BlockSpec(square, lambda j, t: (j, 0, 0)), SMEM),
            ),
            compiler_params=params(),
            name=f"pairs_{d}",
        )(table, own, below, later, *tables)
        home_tags.append(lane_tags)
        if d == 0:
            tags.append(lane_tags)
            codes.append(lane_codes)
        else:
            tags.append(rotated(lane_tags, "tile", d))
            codes.append(rotated(lane_codes, "tile", d))

    surfaces, peaks = pl.pallas_call(
        functools.partial(settle_kernel, shifts, per),
        out_shape=(
            SDS((slots // 2, length, length), jnp.float32),
            SDS((slots,), jnp.float32),
        ),
        in_specs=[SMEM] + [SMEM] * (2 * tiles) + [VMEM] * tiles,
        out_specs=(VMEM, SMEM),
        compiler_params=params(),
        name="settle",
    )(table, *home_tags, *tags, *codes)
    return surfaces[None, None], peaks[None, None]


def solution(mesh):
    in_specs = (
        P(("groups", "sect"), "tile", "half", None, None),
        P(None, ("groups", "sect"), "tile", "half"),
        P(None, ("groups", "sect"), "tile", "half"),
    )
    out_specs = (
        P(("groups", "sect"), "tile", "half", None, None),
        P(("groups", "sect"), "tile", "half"),
    )
    return jax.shard_map(body, mesh=mesh, in_specs=in_specs, out_specs=out_specs, check_vma=False)
```

```python
import functools

import jax
import jax.numpy as jnp
import ml_dtypes
import numpy as np
from jax import lax
from jax.experimental import pallas as pl
from jax.experimental.pallas import tpu as pltpu
from jax.sharding import PartitionSpec as P

FLOOR = 0.05
TOP = 32700.0
STEPS = 8.0
HEAD = 16
SETTLE = 200_000_000
HALF = 16384.0
TINY = 1e-28
LIMIT = 48 * 1024 * 1024

ANY = pl.BlockSpec(memory_space=pl.ANY)
SMEM = pl.BlockSpec(memory_space=pltpu.SMEM)
VMEM = pl.BlockSpec(memory_space=pltpu.VMEM)
SDS = jax.ShapeDtypeStruct


def shifted(value, axis, steps):
    count = lax.axis_size(axis)
    pairs = [(i, i + steps) for i in range(count) if 0 <= i + steps < count]
    return lax.ppermute(value, axis, pairs)


def rotated(value, axis, steps):
    count = lax.axis_size(axis)
    return lax.ppermute(value, axis, [(i, (i + steps) % count) for i in range(count)])


def packed_table(length):
    half = length // 2
    n = np.arange(length)[:, None]
    v = np.arange(half + 1)[None, :]
    angle = 2.0 * np.pi * ((n * v) % length) / length
    table = np.concatenate([np.cos(angle), np.sin(angle[:, 1:half])], axis=1)
    high = table.astype(np.float32).astype(ml_dtypes.bfloat16)
    low = (table - high.astype(np.float64)).astype(np.float32).astype(ml_dtypes.bfloat16)
    return high, low


def dot(left, right):
    return jnp.dot(left, right, preferred_element_type=jnp.float32)


def pieces(value):
    high = value.astype(jnp.bfloat16)
    low = (value - high.astype(jnp.float32)).astype(jnp.bfloat16)
    return high, low


def two_lines(packed, half, row, col, edge):
    cp, cq = packed[:half, :half], packed[:half, half:]
    sp, sq = packed[half:, :half], packed[half:, half:]
    sq_in = jnp.where(edge, 0.0, sq)
    re1 = cp - sq_in
    im1 = -(jnp.where(row, 0.0, sp) + jnp.where(col, 0.0, cq))
    re2 = jnp.where(row, sp, jnp.where(col, cq, cp + sq))
    im2 = jnp.where(edge, -sq, sp - cq)
    return re1, im1, re2, im2


def normalized_packed(one, two, length):
    half = length // 2
    floor = FLOOR * length * length
    rows = lax.broadcasted_iota(jnp.int32, (half, half), 0)
    cols = lax.broadcasted_iota(jnp.int32, (half, half), 1)
    row, col = rows == 0, cols == 0
    edge, corner = row | col, row & col
    a_re1, a_im1, a_re2, a_im2 = two_lines(one, half, row, col, edge)
    b_re1, b_im1, b_re2, b_im2 = two_lines(two, half, row, col, edge)

    def scaled(a_re, a_im, b_re, b_im):
        re = a_re * b_re + a_im * b_im
        im = a_im * b_re - a_re * b_im
        factor = jnp.minimum(lax.rsqrt(re * re + im * im), 1.0 / floor)
        return re * factor, im * factor

    n_re1, n_im1 = scaled(a_re1, a_im1, b_re1, b_im1)
    n_re2, n_im2 = scaled(a_re2, a_im2, b_re2, b_im2)

    def real_corner(value, start_row, start_col):
        a = one[start_row : start_row + half, start_col : start_col + half]
        b = two[start_row : start_row + half, start_col : start_col + half]
        product = a * b
        alone = 0.5 * product / jnp.maximum(jnp.abs(product), floor)
        return jnp.where(corner, alone, value)

    cp = jnp.where(edge, n_re1, n_re1 + n_re2)
    cq = jnp.where(row, -n_im1, jnp.where(col, n_re2, -(n_im1 + n_im2)))
    sp = jnp.where(row, n_re2, jnp.where(col, -n_im1, n_im2 - n_im1))
    sq = jnp.where(edge, -n_im2, n_re2 - n_re1)
    cp = real_corner(cp, 0, 0)
    cq = real_corner(cq, 0, half)
    sp = real_corner(sp, half, 0)
    sq = real_corner(sq, half, half)
    packed = jnp.concatenate(
        [jnp.concatenate([cp, cq], axis=1), jnp.concatenate([sp, sq], axis=1)], axis=0
    )
    return packed * (2.0 / length)


def lanes_kernel(tiles, per, pairs, plan, table):
    slots = pairs.shape[-1]
    me = lax.axis_index("tile")
    for lane in range(tiles * per):
        table[0, lane] = -1
        for field in range(1, 3):
            table[field, lane] = 0
        for field in range(3, 5):
            table[field, lane] = -1
    targets = [plan[0, 0, 0, k] for k in range(slots)]
    for k, target in enumerate(targets):
        rank = jnp.int32(0)
        for earlier in targets[:k]:
            rank += (earlier == target).astype(jnp.int32)
        distance = lax.rem(target - me + tiles, tiles)
        lane = distance * per + rank

        @pl.when(target >= 0)
        def _():
            for field in range(3):
                table[field, lane] = pairs[field, 0, 0, k]
            table[3, lane] = plan[1, 0, 0, k]
            table[4, lane] = k


def gather_kernel(lanes_of, *refs):
    count = len(lanes_of)
    tables, patches = refs[1 : count + 1], refs[count + 1]
    *sent, token = refs[-count - 1 :]
    token[0] = 0
    for table, wanted, out in zip(tables, lanes_of, sent):
        for i, (field, lane) in enumerate(wanted):
            out[i] = patches[table[field, lane]]


def correlate(firsts, seconds, places, guests, th, tl, sh, sl, codes, peaks):
    length = codes.shape[-1]
    per = len(firsts)
    packed = [dot(p, th[...]) + dot(p, tl[...]) for p in firsts + seconds]
    packed = [pieces(p) for p in packed]
    packed = [dot(sh[...], h) + dot(sh[...], w) + dot(sl[...], h) for h, w in packed]
    both = [normalized_packed(packed[j], packed[per + j], length) for j in range(per)]
    both = [pieces(p) for p in both]
    both = [dot(th[...], h) + dot(th[...], w) + dot(tl[...], h) for h, w in both]
    both = [pieces(p) for p in both]
    both = [dot(h, sh[...]) + dot(h, sl[...]) + dot(w, sh[...]) for h, w in both]
    cols = lax.broadcasted_iota(jnp.int32, (HEAD, length), 1)
    head = guest_head(guests, length)
    for j, surface in enumerate(both):
        peaks[j] = jnp.max(surface)
        size = jnp.max(jnp.max(jnp.abs(surface), axis=0, keepdims=True), axis=1, keepdims=True)
        step = jnp.ceil(STEPS * jnp.log2(jnp.maximum(size, TINY)))
        grown = jnp.abs(surface) * (TOP * TOP * jnp.exp2(step * (-1.0 / STEPS)))
        root = grown * lax.rsqrt(jnp.maximum(grown, TINY))
        whole = (root + 0.5).astype(jnp.int32)
        whole = jnp.where(surface < 0, -whole, whole)
        codes[j * length : (j + 1) * length] = whole.astype(jnp.int16)
        head = jnp.where(cols == j, step.astype(jnp.int32), head)
        head = jnp.where(cols == per + j, places[j], head)
    codes[per * length :] = head.astype(jnp.int16)


def guest_head(guests, length):
    cols = lax.broadcasted_iota(jnp.int32, (HEAD, length), 1)
    head = jnp.zeros((HEAD, length), jnp.int32)
    if guests is None:
        return head
    per = guests.shape[0]
    for j in range(per):
        peak = jnp.full((HEAD, length), guests[j])
        power = jnp.ceil(jnp.log2(jnp.maximum(jnp.abs(peak), TINY)))
        share = peak * jnp.exp2(-power) * HALF
        high = share.astype(jnp.int32)
        low = ((share - high.astype(jnp.float32)) * HALF).astype(jnp.int32)
        for i, part in enumerate((power.astype(jnp.int32), high, low)):
            head = jnp.where(cols == 2 * per + 3 * j + i, part, head)
    return head


def guest_peak(head, per, j):
    cols = lax.broadcasted_iota(jnp.int32, head.shape, 1)

    def part(i):
        one = jnp.where(cols == 2 * per + 3 * j + i, head, 0)[:1]
        return jnp.sum(one.astype(jnp.float32), axis=1, keepdims=True)

    return jnp.max((part(1) + part(2) * (1.0 / HALF)) * (1.0 / HALF) * jnp.exp2(part(0)))


def any_of(flags):
    some = flags[0]
    for flag in flags[1:]:
        some = some | flag
    return some


def pair_kernel(lanes, at_below, at_later, live_kind, with_guests, table, before, own, *refs):
    per = len(lanes)
    at_hand = refs[1:3]
    guests = refs[0] if with_guests else None
    th, tl, sh, sl = refs[3:7]
    codes, peaks = refs[-2:]
    kinds = [table[0, lane] for lane in lanes]
    for j in range(per):
        peaks[j] = 0.0
    codes[per * codes.shape[-1] :] = guest_head(guests, codes.shape[-1]).astype(jnp.int16)
    wanted = [k >= 0 if live_kind is None else k == live_kind for k in kinds]

    @pl.when(any_of(wanted))
    def _():
        places = [jnp.where(w, table[3, lane] + 1, 0) for w, lane in zip(wanted, lanes)]
        firsts = [own[table[1, lane]] for lane in lanes]
        seconds = [at_hand[1][at_later + j] for j in range(per)]
        if live_kind is None:
            seconds = [
                jnp.where(kinds[j] == 0, at_hand[0][at_below + j], seconds[j]) for j in range(per)
            ]
        correlate(firsts, seconds, places, guests, th, tl, sh, sl, codes, peaks)


def near_kernel(
    lanes, table, table_above, token, own, up, later, th, tl, sh, sl, codes, peaks, visit_codes, visit_peaks
):
    pair_kernel(
        lanes, 0, 0, 1, False, table, token, own, None, None, later, th, tl, sh, sl, codes, peaks
    )
    per = len(lanes)
    row = lax.axis_index("tile")
    for j in range(per):
        visit_peaks[j] = 0.0
    length = codes.shape[-1]
    visit_codes[per * length :] = jnp.zeros((HEAD, length), jnp.int32).astype(jnp.int16)
    kinds = [table_above[0, lane] for lane in lanes]

    @pl.when((row > 0) & any_of([kind == 0 for kind in kinds]))
    def _():
        firsts = [up[j] for j in range(per)]
        seconds = [own[table_above[2, lane]] for lane in lanes]
        places = [
            jnp.where(kind == 0, table_above[3, lane] + 1, 0) for kind, lane in zip(kinds, lanes)
        ]
        correlate(
            firsts, seconds, places, None, th, tl, sh, sl, visit_codes, visit_peaks
        )


def settle_kernel(per, count, blank, before, *refs):
    codes = refs[:count]
    surfaces, token, room, sems = refs[-4:]
    length = surfaces.shape[-1]
    total = count * per
    token[0] = 0.0
    if blank:
        room[total] = jnp.zeros((length, length), jnp.float32)
        fills = [
            pltpu.make_async_copy(room.at[total], surfaces.at[k], sems.at[total + k])
            for k in range(surfaces.shape[0])
        ]
        for fill in fills:
            fill.start()
        for fill in fills:
            fill.wait()
    cols = lax.broadcasted_iota(jnp.int32, (HEAD, length), 1)
    wanted, copies = [], []
    for i, coded in enumerate(codes):
        head = coded[per * length :].astype(jnp.int32)
        for j in range(per):
            k = i * per + j
            place = jnp.max(jnp.where(cols == per + j, head, 0))
            wanted.append(place > 0)
            target = jnp.maximum(place - 1, 0)
            copies.append(pltpu.make_async_copy(room.at[k], surfaces.at[target], sems.at[k]))
    for i, coded in enumerate(codes):
        for j in range(per):
            k = i * per + j

            @pl.when(wanted[k])
            def _():
                head = coded[per * length :].astype(jnp.int32)
                step = jnp.where(cols == j, head, -(1 << 15))[:1].astype(jnp.float32)
                scale = jnp.exp2(jnp.max(step, axis=1, keepdims=True) * (1.0 / STEPS))
                value = coded[j * length : (j + 1) * length].astype(jnp.int32).astype(jnp.float32)
                room[k] = value * jnp.abs(value) * (scale * (1.0 / (TOP * TOP)))
                copies[k].start()

    for k in range(total):

        @pl.when(wanted[k])
        def _():
            copies[k].wait()


def settle_peaks_kernel(tiles, per, count, before, *refs):
    codes, table, home_peaks = refs[:count], refs[count], refs[count + 1 : count + 1 + tiles]
    surfaces, peaks, token, room, sems = refs[-5:]
    settle_kernel(per, count, False, before, *codes, surfaces, token, room, sems)
    head = codes[-1][per * surfaces.shape[-1] :].astype(jnp.int32)
    back_peaks = [guest_peak(head, per, j) for j in range(per)]
    for k in range(peaks.shape[0]):
        peaks[k] = 0.0
    for d in range(tiles):
        for j in range(per):
            lane = d * per + j
            slot = table[4, lane]
            peak = home_peaks[d][j]
            if d == 1:
                peak = jnp.where(table[0, lane] == 0, back_peaks[j], peak)

            @pl.when(slot >= 0)
            def _():
                peaks[slot] = peak


def params():
    return pltpu.CompilerParams(vmem_limit_bytes=LIMIT)


def cost(flops=1):
    return pl.CostEstimate(flops=flops, bytes_accessed=1, transcendentals=0)


def body(patches, pair_lists, move_plan):
    own = patches[0, 0]
    length = own.shape[-1]
    slots = pair_lists.shape[-1]
    tiles = lax.axis_size("tile")
    per = (slots + tiles - 1) // tiles
    up_one = tiles - 1
    far = sorted(range(2, up_one), key=lambda d: -min(d, tiles - d))
    groups_below = [far, [up_one, 0]]
    groups_later = [far, [1, up_one], [0]]

    def lanes_at(d):
        return [d * per + j for j in range(per)]

    def call(kernel, name, outs, *operands, last=()):
        return pl.pallas_call(
            kernel,
            out_shape=outs,
            in_specs=[VMEM if o.dtype in (own.dtype, jnp.int16) else SMEM for o in operands]
            + [ANY] * len(last),
            out_specs=jax.tree.map(lambda o: SMEM if len(o.shape) == 1 else VMEM, outs),
            compiler_params=params(),
            cost_estimate=cost(),
            name=name,
        )(*operands, *last)

    def picked(name, token, wanted, *arrived):
        lists = [[(f, lane) for d in ds for lane in lanes_at(d)] for _, f, ds in wanted]
        outs = tuple(SDS((len(w), length, length), own.dtype) for w in lists)
        tables = [t for t, _, _ in wanted]
        *sent, token = call(
            functools.partial(gather_kernel, lists),
            name,
            outs + (SDS((1,), jnp.int32),),
            token,
            *tables,
            own,
            last=arrived,
        )
        return sent, token

    table = pl.pallas_call(
        functools.partial(lanes_kernel, tiles, per),
        out_shape=SDS((5, tiles * per), jnp.int32),
        in_specs=[SMEM, SMEM],
        out_specs=SMEM,
        name="lanes",
    )(pair_lists, move_plan)
    table_above = shifted(table, "tile", 1)
    table_before = shifted(table, "sect", 1)
    (first_up, below_0, later_0), token = picked(
        "gather_first",
        table,
        [(table, 1, [1]), (table_above, 2, groups_below[0]), (table_before, 2, groups_later[0])],
    )
    up = shifted(first_up, "tile", 1)
    below_0, later_0 = shifted(below_0, "tile", -1), shifted(later_0, "sect", -1)
    (below_1, later_1, later_2), token = picked(
        "gather_last",
        token,
        [(table_above, 2, groups_below[1])] + [(table_before, 2, g) for g in groups_later[1:]],
        below_0,
        later_0,
        up,
    )
    below = [below_0, shifted(below_1, "tile", -1)]
    later = [later_0, shifted(later_1, "sect", -1), shifted(later_2, "sect", -1)]

    high, low = packed_table(length)
    tables = [jnp.asarray(t) for t in (high, low, high.T.copy(), low.T.copy())]
    result = (SDS((per * length + HEAD, length), jnp.int16), SDS((per,), jnp.float32))

    works = slots // 2
    surfaces_kind, token_kind = SDS((works, length, length), jnp.float32), SDS((1,), jnp.float32)
    peaks_kind = SDS((slots,), jnp.float32)

    def settled(name, all_codes, before, surfaces=None, table=None, home_peaks=()):
        count = len(all_codes)
        extra = ([] if table is None else [table]) + list(home_peaks)
        blank = surfaces is None
        kernel = functools.partial(settle_kernel, per, count, blank)
        if extra:
            kernel = functools.partial(settle_peaks_kernel, tiles, per, count)
        return pl.pallas_call(
            kernel,
            out_shape=(surfaces_kind,) + ((peaks_kind,) if extra else ()) + (token_kind,),
            in_specs=[SMEM] + [VMEM] * count + [SMEM] * len(extra) + ([] if blank else [ANY]),
            out_specs=(ANY,) + ((SMEM,) if extra else ()) + (SMEM,),
            scratch_shapes=[
                pltpu.VMEM((count * per + 1, length, length), jnp.float32),
                pltpu.SemaphoreType.DMA((count * per + works,)),
            ],
            input_output_aliases={} if blank else {1 + count + len(extra): 0},
            compiler_params=params(),
            cost_estimate=cost(SETTLE),
            name=name,
        )(before, *all_codes, *extra, *([] if blank else [surfaces]))

    home_peaks, moving = [None] * tiles, {}

    def paired(d, before, guests, near, late, last=()):
        lane_codes, home_peaks[d] = call(
            functools.partial(
                pair_kernel,
                lanes_at(d),
                groups_below[near].index(d) * per,
                groups_later[late].index(d) * per,
                None,
                d == up_one,
            ),
            f"pairs_{d}",
            result,
            table,
            before,
            own,
            guests,
            below[near],
            later[late],
            *tables,
            last=last,
        )
        moving[d] = lane_codes if d == 0 else rotated(lane_codes, "tile", d)
        return home_peaks[d]

    for d in far:
        token = paired(d, token, token, 0, 0)
    lane_codes, home_peaks[1], visit_codes, guests = call(
        functools.partial(near_kernel, lanes_at(1)),
        "pairs_1",
        result + result,
        table,
        table_above,
        token,
        own,
        up,
        later[1],
        *tables,
    )
    moving[1] = rotated(lane_codes, "tile", 1)
    surfaces, before = settled("settle_visit", [visit_codes], guests)
    before = paired(up_one, before, guests, 1, 1, last=[later[2]])
    before = paired(0, before, before, 1, 2)
    early = [moving[d] for d in [0] + far]
    surfaces, before = settled("settle_early", early, before, surfaces)
    surfaces, before = settled("settle_1", [moving[1]], before, surfaces)
    surfaces, peaks, _ = settled(
        "settle_last", [moving[up_one]], before, surfaces, table, home_peaks
    )
    return surfaces[None, None], peaks[None, None]


def solution(mesh):
    in_specs = (
        P(("groups", "sect"), "tile", "half", None, None),
        P(None, ("groups", "sect"), "tile", "half"),
        P(None, ("groups", "sect"), "tile", "half"),
    )
    out_specs = (
        P(("groups", "sect"), "tile", "half", None, None),
        P(("groups", "sect"), "tile", "half"),
    )
    return jax.shard_map(body, mesh=mesh, in_specs=in_specs, out_specs=out_specs, check_vma=False)
```

```python
import functools

import jax
import jax.numpy as jnp
import ml_dtypes
import numpy as np
from jax import lax
from jax.experimental import pallas as pl
from jax.experimental.pallas import tpu as pltpu
from jax.sharding import PartitionSpec as P

FLOOR = 0.05
TOP = 32700.0
STEPS = 8.0
HEAD = 16
LANES = 4_000_000_000
FIRST = 35_000_000_000
SETTLE = 200_000_000
HALF = 16384.0
TINY = 1e-28
LIMIT = 48 * 1024 * 1024

ANY = pl.BlockSpec(memory_space=pl.ANY)
SMEM = pl.BlockSpec(memory_space=pltpu.SMEM)
VMEM = pl.BlockSpec(memory_space=pltpu.VMEM)
SDS = jax.ShapeDtypeStruct


def shifted(value, axis, steps):
    count = lax.axis_size(axis)
    pairs = [(i, i + steps) for i in range(count) if 0 <= i + steps < count]
    return lax.ppermute(value, axis, pairs)


def rotated(value, axis, steps):
    count = lax.axis_size(axis)
    return lax.ppermute(value, axis, [(i, (i + steps) % count) for i in range(count)])


def packed_table(length):
    half = length // 2
    n = np.arange(length)[:, None]
    v = np.arange(half + 1)[None, :]
    angle = 2.0 * np.pi * ((n * v) % length) / length
    table = np.concatenate([np.cos(angle), np.sin(angle[:, 1:half])], axis=1)
    high = table.astype(np.float32).astype(ml_dtypes.bfloat16)
    low = (table - high.astype(np.float64)).astype(np.float32).astype(ml_dtypes.bfloat16)
    return high, low


def dot(left, right):
    return jnp.dot(left, right, preferred_element_type=jnp.float32)


def pieces(value):
    high = value.astype(jnp.bfloat16)
    low = (value - high.astype(jnp.float32)).astype(jnp.bfloat16)
    return high, low


def two_lines(packed, half, row, col, edge):
    cp, cq = packed[:half, :half], packed[:half, half:]
    sp, sq = packed[half:, :half], packed[half:, half:]
    sq_in = jnp.where(edge, 0.0, sq)
    re1 = cp - sq_in
    im1 = -(jnp.where(row, 0.0, sp) + jnp.where(col, 0.0, cq))
    re2 = jnp.where(row, sp, jnp.where(col, cq, cp + sq))
    im2 = jnp.where(edge, -sq, sp - cq)
    return re1, im1, re2, im2


def normalized_packed(one, two, length):
    half = length // 2
    floor = FLOOR * length * length
    rows = lax.broadcasted_iota(jnp.int32, (half, half), 0)
    cols = lax.broadcasted_iota(jnp.int32, (half, half), 1)
    row, col = rows == 0, cols == 0
    edge, corner = row | col, row & col
    a_re1, a_im1, a_re2, a_im2 = two_lines(one, half, row, col, edge)
    b_re1, b_im1, b_re2, b_im2 = two_lines(two, half, row, col, edge)

    def scaled(a_re, a_im, b_re, b_im):
        re = a_re * b_re + a_im * b_im
        im = a_im * b_re - a_re * b_im
        factor = jnp.minimum(lax.rsqrt(re * re + im * im), 1.0 / floor)
        return re * factor, im * factor

    n_re1, n_im1 = scaled(a_re1, a_im1, b_re1, b_im1)
    n_re2, n_im2 = scaled(a_re2, a_im2, b_re2, b_im2)

    def real_corner(value, start_row, start_col):
        a = one[start_row : start_row + half, start_col : start_col + half]
        b = two[start_row : start_row + half, start_col : start_col + half]
        product = a * b
        alone = 0.5 * product / jnp.maximum(jnp.abs(product), floor)
        return jnp.where(corner, alone, value)

    cp = jnp.where(edge, n_re1, n_re1 + n_re2)
    cq = jnp.where(row, -n_im1, jnp.where(col, n_re2, -(n_im1 + n_im2)))
    sp = jnp.where(row, n_re2, jnp.where(col, -n_im1, n_im2 - n_im1))
    sq = jnp.where(edge, -n_im2, n_re2 - n_re1)
    cp = real_corner(cp, 0, 0)
    cq = real_corner(cq, 0, half)
    sp = real_corner(sp, half, 0)
    sq = real_corner(sq, half, half)
    packed = jnp.concatenate(
        [jnp.concatenate([cp, cq], axis=1), jnp.concatenate([sp, sq], axis=1)], axis=0
    )
    return packed * (2.0 / length)


def lanes_kernel(tiles, per, pairs, plan, table):
    slots = pairs.shape[-1]
    me = lax.axis_index("tile")
    for lane in range(tiles * per):
        table[0, lane] = -1
        for field in range(1, 3):
            table[field, lane] = 0
        for field in range(3, 5):
            table[field, lane] = -1
    targets = [plan[0, 0, 0, k] for k in range(slots)]
    for k, target in enumerate(targets):
        rank = jnp.int32(0)
        for earlier in targets[:k]:
            rank += (earlier == target).astype(jnp.int32)
        distance = lax.rem(target - me + tiles, tiles)
        lane = distance * per + rank

        @pl.when(target >= 0)
        def _():
            for field in range(3):
                table[field, lane] = pairs[field, 0, 0, k]
            table[3, lane] = plan[1, 0, 0, k]
            table[4, lane] = k


def gather_kernel(lanes_of, *refs):
    count = len(lanes_of)
    tables, patches = refs[1 : count + 1], refs[count + 1]
    *sent, token = refs[-count - 1 :]
    for at in np.ndindex(*token.shape):
        token[at] = refs[0][at]
    for table, wanted, out in zip(tables, lanes_of, sent):
        for i, (field, lane) in enumerate(wanted):
            out[i] = patches[table[field, lane]]


def correlate(firsts, seconds, places, guests, th, tl, sh, sl, codes, peaks):
    length = codes.shape[-1]
    per = len(firsts)
    packed = [dot(p, th[...]) + dot(p, tl[...]) for p in firsts + seconds]
    packed = [pieces(p) for p in packed]
    packed = [dot(sh[...], h) + dot(sh[...], w) + dot(sl[...], h) for h, w in packed]
    both = [normalized_packed(packed[j], packed[per + j], length) for j in range(per)]
    both = [pieces(p) for p in both]
    both = [dot(th[...], h) + dot(th[...], w) + dot(tl[...], h) for h, w in both]
    both = [pieces(p) for p in both]
    both = [dot(h, sh[...]) + dot(h, sl[...]) + dot(w, sh[...]) for h, w in both]
    cols = lax.broadcasted_iota(jnp.int32, (HEAD, length), 1)
    head = guest_head(guests, length)
    for j, surface in enumerate(both):
        peaks[j] = jnp.max(surface)
        size = jnp.max(jnp.max(jnp.abs(surface), axis=0, keepdims=True), axis=1, keepdims=True)
        step = jnp.ceil(STEPS * jnp.log2(jnp.maximum(size, TINY)))
        grown = jnp.abs(surface) * (TOP * TOP * jnp.exp2(step * (-1.0 / STEPS)))
        root = grown * lax.rsqrt(jnp.maximum(grown, TINY))
        whole = (root + 0.5).astype(jnp.int32)
        whole = jnp.where(surface < 0, -whole, whole)
        codes[j * length : (j + 1) * length] = whole.astype(jnp.int16)
        head = jnp.where(cols == j, step.astype(jnp.int32), head)
        head = jnp.where(cols == per + j, places[j], head)
    codes[per * length : per * length + HEAD] = head.astype(jnp.int16)


def guest_head(guests, length):
    cols = lax.broadcasted_iota(jnp.int32, (HEAD, length), 1)
    head = jnp.zeros((HEAD, length), jnp.int32)
    if guests is None:
        return head
    per = guests.shape[0]
    for j in range(per):
        peak = jnp.full((HEAD, length), guests[j])
        power = jnp.ceil(jnp.log2(jnp.maximum(jnp.abs(peak), TINY)))
        share = peak * jnp.exp2(-power) * HALF
        high = share.astype(jnp.int32)
        low = ((share - high.astype(jnp.float32)) * HALF).astype(jnp.int32)
        for i, part in enumerate((power.astype(jnp.int32), high, low)):
            head = jnp.where(cols == 2 * per + 3 * j + i, part, head)
    return head


def guest_peak(head, per, j):
    cols = lax.broadcasted_iota(jnp.int32, head.shape, 1)

    def part(i):
        one = jnp.where(cols == 2 * per + 3 * j + i, head, 0)[:1]
        return jnp.sum(one.astype(jnp.float32), axis=1, keepdims=True)

    return jnp.max((part(1) + part(2) * (1.0 / HALF)) * (1.0 / HALF) * jnp.exp2(part(0)))


def any_of(flags):
    some = flags[0]
    for flag in flags[1:]:
        some = some | flag
    return some


def pair_kernel(lanes, at_below, at_later, live_kind, with_guests, table, before, own, *refs):
    per = len(lanes)
    at_hand = refs[1:3]
    guests = refs[0] if with_guests else None
    th, tl, sh, sl = refs[3:7]
    codes, peaks = refs[-2:]
    kinds = [table[0, lane] for lane in lanes]
    for j in range(per):
        peaks[j] = 0.0
    codes[per * codes.shape[-1] : per * codes.shape[-1] + HEAD] = guest_head(guests, codes.shape[-1]).astype(jnp.int16)
    wanted = [k >= 0 if live_kind is None else k == live_kind for k in kinds]

    @pl.when(any_of(wanted))
    def _():
        places = [jnp.where(w, table[3, lane] + 1, 0) for w, lane in zip(wanted, lanes)]
        firsts = [own[table[1, lane]] for lane in lanes]
        seconds = [at_hand[1][at_later + j] for j in range(per)]
        if live_kind is None:
            seconds = [
                jnp.where(kinds[j] == 0, at_hand[0][at_below + j], seconds[j]) for j in range(per)
            ]
        correlate(firsts, seconds, places, guests, th, tl, sh, sl, codes, peaks)


def visit_kernel(lanes, table_above, token, own, up, th, tl, sh, sl, _, codes, peaks):
    per = len(lanes)
    length = codes.shape[-1]
    row = lax.axis_index("tile")
    for j in range(per):
        peaks[j] = 0.0
    codes[per * length : per * length + HEAD] = jnp.zeros((HEAD, length), jnp.int32).astype(jnp.int16)
    kinds = [table_above[0, lane] for lane in lanes]

    @pl.when((row > 0) & any_of([kind == 0 for kind in kinds]))
    def _():
        firsts = [up[j] for j in range(per)]
        seconds = [own[table_above[2, lane]] for lane in lanes]
        places = [
            jnp.where(kind == 0, table_above[3, lane] + 1, 0) for kind, lane in zip(kinds, lanes)
        ]
        correlate(firsts, seconds, places, None, th, tl, sh, sl, codes, peaks)


def settle_kernel(per, count, blank, before, *refs):
    codes = refs[:count]
    surfaces, token, room, sems = refs[-4:]
    length = surfaces.shape[-1]
    total = count * per
    token[0] = 0.0
    if blank:
        room[total] = jnp.zeros((length, length), jnp.float32)
        fills = [
            pltpu.make_async_copy(room.at[total], surfaces.at[k], sems.at[total + k])
            for k in range(surfaces.shape[0])
        ]
        for fill in fills:
            fill.start()
        for fill in fills:
            fill.wait()
    cols = lax.broadcasted_iota(jnp.int32, (HEAD, length), 1)
    wanted, copies = [], []
    for i, coded in enumerate(codes):
        head = coded[per * length : per * length + HEAD].astype(jnp.int32)
        for j in range(per):
            k = i * per + j
            place = jnp.max(jnp.where(cols == per + j, head, 0))
            wanted.append(place > 0)
            target = jnp.maximum(place - 1, 0)
            copies.append(pltpu.make_async_copy(room.at[k], surfaces.at[target], sems.at[k]))
    for i, coded in enumerate(codes):
        for j in range(per):
            k = i * per + j

            @pl.when(wanted[k])
            def _():
                head = coded[per * length : per * length + HEAD].astype(jnp.int32)
                step = jnp.where(cols == j, head, -(1 << 15))[:1].astype(jnp.float32)
                scale = jnp.exp2(jnp.max(step, axis=1, keepdims=True) * (1.0 / STEPS))
                value = coded[j * length : (j + 1) * length].astype(jnp.int32).astype(jnp.float32)
                room[k] = value * jnp.abs(value) * (scale * (1.0 / (TOP * TOP)))
                copies[k].start()

    for k in range(total):

        @pl.when(wanted[k])
        def _():
            copies[k].wait()


def settle_peaks_kernel(tiles, per, count, before, *refs):
    codes, table, home_peaks = refs[:count], refs[count], refs[count + 1 : count + 1 + tiles]
    surfaces, peaks, token, room, sems = refs[-5:]
    settle_kernel(per, count, False, before, *codes, surfaces, token, room, sems)
    head = codes[-1][per * surfaces.shape[-1] : per * surfaces.shape[-1] + HEAD].astype(jnp.int32)
    back_peaks = [guest_peak(head, per, j) for j in range(per)]
    for k in range(peaks.shape[0]):
        peaks[k] = 0.0
    for d in range(tiles):
        for j in range(per):
            lane = d * per + j
            slot = table[4, lane]
            peak = home_peaks[d][j]
            if d == 1:
                peak = jnp.where(table[0, lane] == 0, back_peaks[j], peak)

            @pl.when(slot >= 0)
            def _():
                peaks[slot] = peak


def params():
    return pltpu.CompilerParams(vmem_limit_bytes=LIMIT)


def cost(flops=1):
    return pl.CostEstimate(flops=flops, bytes_accessed=1, transcendentals=0)


def body(patches, pair_lists, move_plan):
    own = patches[0, 0]
    length = own.shape[-1]
    slots = pair_lists.shape[-1]
    tiles = lax.axis_size("tile")
    per = (slots + tiles - 1) // tiles
    up_one = tiles - 1
    far = sorted(range(2, up_one), key=lambda d: -min(d, tiles - d))
    groups_below = [far + [up_one], [0]]
    groups_later = [far, [1], [up_one], [0]]

    def lanes_at(d):
        return [d * per + j for j in range(per)]

    def call(kernel, name, outs, *operands, last=(), flops=SETTLE):
        return pl.pallas_call(
            kernel,
            out_shape=outs,
            in_specs=[VMEM if o.dtype in (own.dtype, jnp.int16) else SMEM for o in operands]
            + [ANY] * len(last),
            out_specs=jax.tree.map(lambda o: SMEM if len(o.shape) == 1 or o.dtype == jnp.int32 else VMEM, outs),
            compiler_params=params(),
            cost_estimate=cost(flops),
            name=name,
        )(*operands, *last)

    def picked(name, token, wanted, *arrived):
        lists = [[(f, lane) for d in ds for lane in lanes_at(d)] for _, f, ds in wanted]
        outs = tuple(SDS((len(w), length, length), own.dtype) for w in lists)
        tables = [t for t, _, _ in wanted]
        *sent, token = call(
            functools.partial(gather_kernel, lists),
            name,
            outs + (SDS(token.shape, token.dtype),),
            token,
            *tables,
            own,
            last=arrived,
        )
        return sent, token

    table = pl.pallas_call(
        functools.partial(lanes_kernel, tiles, per),
        out_shape=SDS((5, tiles * per), jnp.int32),
        in_specs=[SMEM, SMEM],
        out_specs=SMEM,
        cost_estimate=cost(LANES),
        name="lanes",
    )(pair_lists, move_plan)
    table_above = shifted(table, "tile", 1)
    (below_0,), same_table = picked("gather_below", table, [(table_above, 2, groups_below[0])])
    below_0 = shifted(below_0, "tile", -1)
    table_before = shifted(same_table, "sect", 1)
    (first_up, below_1, later_0), token = picked(
        "gather_later",
        table,
        [(table, 1, [1]), (table_above, 2, groups_below[1]), (table_before, 2, groups_later[0])],
    )
    up, later_0 = shifted(first_up, "tile", 1), shifted(later_0, "sect", -1)
    below = [below_0, shifted(below_1, "tile", -1)]
    (later_1, later_2), token = picked(
        "gather_next", token, [(table_before, 2, g) for g in groups_later[1:3]], later_0, up
    )
    later = [later_0, shifted(later_1, "sect", -1), shifted(later_2, "sect", -1)]

    high, low = packed_table(length)
    tables = [jnp.asarray(t) for t in (high, low, high.T.copy(), low.T.copy())]
    result = (SDS((per * length + HEAD, length), jnp.int16), SDS((per,), jnp.float32))

    longer = (SDS((per * length + 2 * HEAD, length), jnp.int16), result[1])
    works = slots // 2
    surfaces_kind, token_kind = SDS((works, length, length), jnp.float32), SDS((1,), jnp.float32)
    peaks_kind = SDS((slots,), jnp.float32)

    def settled(name, all_codes, before, surfaces=None, table=None, home_peaks=()):
        count = len(all_codes)
        extra = ([] if table is None else [table]) + list(home_peaks)
        blank = surfaces is None
        kernel = functools.partial(settle_kernel, per, count, blank)
        if extra:
            kernel = functools.partial(settle_peaks_kernel, tiles, per, count)
        return pl.pallas_call(
            kernel,
            out_shape=(surfaces_kind,) + ((peaks_kind,) if extra else ()) + (token_kind,),
            in_specs=[SMEM] + [VMEM] * count + [SMEM] * len(extra) + ([] if blank else [ANY]),
            out_specs=(ANY,) + ((SMEM,) if extra else ()) + (SMEM,),
            scratch_shapes=[
                pltpu.VMEM((count * per + 1, length, length), jnp.float32),
                pltpu.SemaphoreType.DMA((count * per + works,)),
            ],
            input_output_aliases={} if blank else {1 + count + len(extra): 0},
            compiler_params=params(),
            cost_estimate=cost(SETTLE),
            name=name,
        )(before, *all_codes, *extra, *([] if blank else [surfaces]))

    home_peaks, moving = [None] * tiles, {}

    def paired(d, before, guests, last=(), flops=SETTLE):
        near = [i for i, g in enumerate(groups_below) if d in g or d == 1][0]
        late = [i for i, g in enumerate(groups_later) if d in g][0]
        lane_codes, home_peaks[d] = call(
            functools.partial(
                pair_kernel,
                lanes_at(d),
                0 if d == 1 else groups_below[near].index(d) * per,
                groups_later[late].index(d) * per,
                1 if d == 1 else None,
                d == up_one,
            ),
            f"pairs_{d}",
            longer if d == 1 else result,
            table,
            before,
            own,
            guests,
            below[near],
            later[late],
            *tables,
            last=last,
            flops=flops,
        )
        moving[d] = lane_codes if d == 0 else rotated(lane_codes, "tile", d)
        return home_peaks[d]

    for d in far:
        token = paired(d, token, token, flops=FIRST)
    (later_3,), _ = picked("gather_home", token, [(table_before, 2, groups_later[3])])
    later.append(shifted(later_3, "sect", -1))
    visit_codes, guests = call(
        functools.partial(visit_kernel, lanes_at(1)),
        "visit",
        result,
        table_above,
        token,
        own,
        up,
        *tables,
        last=[below[1]],
    )
    surfaces, before = settled("settle_visit", [visit_codes], guests)
    before = paired(1, before, before)
    before = paired(up_one, before, guests)
    before = paired(0, before, before)
    early = [moving[d] for d in [0] + far]
    surfaces, before = settled("settle_early", early, before, surfaces)
    last = [moving[1], moving[up_one]]
    surfaces, peaks, _ = settled("settle_last", last, before, surfaces, table, home_peaks)
    return surfaces[None, None], peaks[None, None]


def solution(mesh):
    in_specs = (
        P(("groups", "sect"), "tile", "half", None, None),
        P(None, ("groups", "sect"), "tile", "half"),
        P(None, ("groups", "sect"), "tile", "half"),
    )
    out_specs = (
        P(("groups", "sect"), "tile", "half", None, None),
        P(("groups", "sect"), "tile", "half"),
    )
    return jax.shard_map(body, mesh=mesh, in_specs=in_specs, out_specs=out_specs, check_vma=False)
```

```python
import functools

import jax
import jax.numpy as jnp
import ml_dtypes
import numpy as np
from jax import lax
from jax.experimental import pallas as pl
from jax.experimental.pallas import tpu as pltpu
from jax.sharding import PartitionSpec as P

FLOOR = 0.05
TOP = 32700.0
STEPS = 8.0
HEAD = 16
LANES = 4_000_000_000
FIRST = 35_000_000_000
SETTLE = 200_000_000
HALF = 16384.0
TINY = 1e-28
LIMIT = 48 * 1024 * 1024

ANY = pl.BlockSpec(memory_space=pl.ANY)
SMEM = pl.BlockSpec(memory_space=pltpu.SMEM)
VMEM = pl.BlockSpec(memory_space=pltpu.VMEM)
SDS = jax.ShapeDtypeStruct


def shifted(value, axis, steps):
    count = lax.axis_size(axis)
    pairs = [(i, i + steps) for i in range(count) if 0 <= i + steps < count]
    return lax.ppermute(value, axis, pairs)


def rotated(value, axis, steps):
    count = lax.axis_size(axis)
    return lax.ppermute(value, axis, [(i, (i + steps) % count) for i in range(count)])


def packed_table(length):
    half = length // 2
    n = np.arange(length)[:, None]
    v = np.arange(half + 1)[None, :]
    angle = 2.0 * np.pi * ((n * v) % length) / length
    table = np.concatenate([np.cos(angle), np.sin(angle[:, 1:half])], axis=1)
    high = table.astype(np.float32).astype(ml_dtypes.bfloat16)
    low = (table - high.astype(np.float64)).astype(np.float32).astype(ml_dtypes.bfloat16)
    return high, low


def dot(left, right):
    return jnp.dot(left, right, preferred_element_type=jnp.float32)


def pieces(value):
    high = value.astype(jnp.bfloat16)
    low = (value - high.astype(jnp.float32)).astype(jnp.bfloat16)
    return high, low


def two_lines(packed, half, row, col, edge):
    cp, cq = packed[:half, :half], packed[:half, half:]
    sp, sq = packed[half:, :half], packed[half:, half:]
    sq_in = jnp.where(edge, 0.0, sq)
    re1 = cp - sq_in
    im1 = -(jnp.where(row, 0.0, sp) + jnp.where(col, 0.0, cq))
    re2 = jnp.where(row, sp, jnp.where(col, cq, cp + sq))
    im2 = jnp.where(edge, -sq, sp - cq)
    return re1, im1, re2, im2


def normalized_packed(one, two, length):
    half = length // 2
    floor = FLOOR * length * length
    rows = lax.broadcasted_iota(jnp.int32, (half, half), 0)
    cols = lax.broadcasted_iota(jnp.int32, (half, half), 1)
    row, col = rows == 0, cols == 0
    edge, corner = row | col, row & col
    a_re1, a_im1, a_re2, a_im2 = two_lines(one, half, row, col, edge)
    b_re1, b_im1, b_re2, b_im2 = two_lines(two, half, row, col, edge)

    def scaled(a_re, a_im, b_re, b_im):
        re = a_re * b_re + a_im * b_im
        im = a_im * b_re - a_re * b_im
        factor = jnp.minimum(lax.rsqrt(re * re + im * im), 1.0 / floor)
        return re * factor, im * factor

    n_re1, n_im1 = scaled(a_re1, a_im1, b_re1, b_im1)
    n_re2, n_im2 = scaled(a_re2, a_im2, b_re2, b_im2)

    def real_corner(value, start_row, start_col):
        a = one[start_row : start_row + half, start_col : start_col + half]
        b = two[start_row : start_row + half, start_col : start_col + half]
        product = a * b
        alone = 0.5 * product / jnp.maximum(jnp.abs(product), floor)
        return jnp.where(corner, alone, value)

    cp = jnp.where(edge, n_re1, n_re1 + n_re2)
    cq = jnp.where(row, -n_im1, jnp.where(col, n_re2, -(n_im1 + n_im2)))
    sp = jnp.where(row, n_re2, jnp.where(col, -n_im1, n_im2 - n_im1))
    sq = jnp.where(edge, -n_im2, n_re2 - n_re1)
    cp = real_corner(cp, 0, 0)
    cq = real_corner(cq, 0, half)
    sp = real_corner(sp, half, 0)
    sq = real_corner(sq, half, half)
    packed = jnp.concatenate(
        [jnp.concatenate([cp, cq], axis=1), jnp.concatenate([sp, sq], axis=1)], axis=0
    )
    return packed * (2.0 / length)


def lanes_kernel(tiles, per, pairs, plan, table):
    slots = pairs.shape[-1]
    me = lax.axis_index("tile")
    for lane in range(tiles * per):
        table[0, lane] = -1
        for field in range(1, 3):
            table[field, lane] = 0
        for field in range(3, 5):
            table[field, lane] = -1
    targets = [plan[0, 0, 0, k] for k in range(slots)]
    for k, target in enumerate(targets):
        rank = jnp.int32(0)
        for earlier in targets[:k]:
            rank += (earlier == target).astype(jnp.int32)
        distance = lax.rem(target - me + tiles, tiles)
        lane = distance * per + rank

        @pl.when(target >= 0)
        def _():
            for field in range(3):
                table[field, lane] = pairs[field, 0, 0, k]
            table[3, lane] = plan[1, 0, 0, k]
            table[4, lane] = k


def gather_kernel(lanes_of, *refs):
    count = len(lanes_of)
    tables, patches = refs[1 : count + 1], refs[count + 1]
    *sent, token = refs[-count - 1 :]
    for at in np.ndindex(*token.shape):
        token[at] = refs[0][at]
    for table, wanted, out in zip(tables, lanes_of, sent):
        for i, (field, lane) in enumerate(wanted):
            out[i] = patches[table[field, lane]]


def correlate(firsts, seconds, places, guests, th, tl, sh, sl, codes, peaks):
    length = codes.shape[-1]
    per = len(firsts)
    packed = [dot(p, th[...]) + dot(p, tl[...]) for p in firsts + seconds]
    packed = [pieces(p) for p in packed]
    packed = [dot(sh[...], h) + dot(sh[...], w) + dot(sl[...], h) for h, w in packed]
    both = [normalized_packed(packed[j], packed[per + j], length) for j in range(per)]
    both = [pieces(p) for p in both]
    both = [dot(th[...], h) + dot(th[...], w) + dot(tl[...], h) for h, w in both]
    both = [pieces(p) for p in both]
    both = [dot(h, sh[...]) + dot(h, sl[...]) + dot(w, sh[...]) for h, w in both]
    cols = lax.broadcasted_iota(jnp.int32, (HEAD, length), 1)
    head = guest_head(guests, length)
    for j, surface in enumerate(both):
        peaks[j] = jnp.max(surface)
        size = jnp.max(jnp.max(jnp.abs(surface), axis=0, keepdims=True), axis=1, keepdims=True)
        step = jnp.ceil(STEPS * jnp.log2(jnp.maximum(size, TINY)))
        grown = jnp.abs(surface) * (TOP * TOP * jnp.exp2(step * (-1.0 / STEPS)))
        root = grown * lax.rsqrt(jnp.maximum(grown, TINY))
        whole = (root + 0.5).astype(jnp.int32)
        whole = jnp.where(surface < 0, -whole, whole)
        codes[j * length : (j + 1) * length] = whole.astype(jnp.int16)
        head = jnp.where(cols == j, step.astype(jnp.int32), head)
        head = jnp.where(cols == per + j, places[j], head)
    codes[per * length : per * length + HEAD] = head.astype(jnp.int16)


def guest_head(guests, length):
    cols = lax.broadcasted_iota(jnp.int32, (HEAD, length), 1)
    head = jnp.zeros((HEAD, length), jnp.int32)
    if guests is None:
        return head
    per = guests.shape[0]
    for j in range(per):
        peak = jnp.full((HEAD, length), guests[j])
        power = jnp.ceil(jnp.log2(jnp.maximum(jnp.abs(peak), TINY)))
        share = peak * jnp.exp2(-power) * HALF
        high = share.astype(jnp.int32)
        low = ((share - high.astype(jnp.float32)) * HALF).astype(jnp.int32)
        for i, part in enumerate((power.astype(jnp.int32), high, low)):
            head = jnp.where(cols == 2 * per + 3 * j + i, part, head)
    return head


def guest_peak(head, per, j):
    cols = lax.broadcasted_iota(jnp.int32, head.shape, 1)

    def part(i):
        one = jnp.where(cols == 2 * per + 3 * j + i, head, 0)[:1]
        return jnp.sum(one.astype(jnp.float32), axis=1, keepdims=True)

    return jnp.max((part(1) + part(2) * (1.0 / HALF)) * (1.0 / HALF) * jnp.exp2(part(0)))


def any_of(flags):
    some = flags[0]
    for flag in flags[1:]:
        some = some | flag
    return some


def pair_kernel(lanes, at_below, at_later, live_kind, with_guests, table, before, own, *refs):
    per = len(lanes)
    at_hand = refs[1:3]
    guests = refs[0] if with_guests else None
    th, tl, sh, sl = refs[3:7]
    codes, peaks = refs[-2:]
    kinds = [table[0, lane] for lane in lanes]
    for j in range(per):
        peaks[j] = 0.0
    codes[per * codes.shape[-1] : per * codes.shape[-1] + HEAD] = guest_head(guests, codes.shape[-1]).astype(jnp.int16)
    wanted = [k >= 0 if live_kind is None else k == live_kind for k in kinds]

    @pl.when(any_of(wanted))
    def _():
        places = [jnp.where(w, table[3, lane] + 1, 0) for w, lane in zip(wanted, lanes)]
        firsts = [own[table[1, lane]] for lane in lanes]
        seconds = [at_hand[1][at_later + j] for j in range(per)]
        if live_kind is None:
            seconds = [
                jnp.where(kinds[j] == 0, at_hand[0][at_below + j], seconds[j]) for j in range(per)
            ]
        correlate(firsts, seconds, places, guests, th, tl, sh, sl, codes, peaks)


def visit_kernel(lanes, table_above, token, own, up, th, tl, sh, sl, _, codes, peaks):
    per = len(lanes)
    length = codes.shape[-1]
    row = lax.axis_index("tile")
    for j in range(per):
        peaks[j] = 0.0
    codes[per * length : per * length + HEAD] = jnp.zeros((HEAD, length), jnp.int32).astype(jnp.int16)
    kinds = [table_above[0, lane] for lane in lanes]

    @pl.when((row > 0) & any_of([kind == 0 for kind in kinds]))
    def _():
        firsts = [up[j] for j in range(per)]
        seconds = [own[table_above[2, lane]] for lane in lanes]
        places = [
            jnp.where(kind == 0, table_above[3, lane] + 1, 0) for kind, lane in zip(kinds, lanes)
        ]
        correlate(firsts, seconds, places, None, th, tl, sh, sl, codes, peaks)


def settle_kernel(per, count, blank, before, *refs):
    codes = refs[:count]
    surfaces, token, room, sems = refs[-4:]
    length = surfaces.shape[-1]
    total = count * per
    token[0] = 0.0
    if blank:
        room[total] = jnp.zeros((length, length), jnp.float32)
        fills = [
            pltpu.make_async_copy(room.at[total], surfaces.at[k], sems.at[total + k])
            for k in range(surfaces.shape[0])
        ]
        for fill in fills:
            fill.start()
        for fill in fills:
            fill.wait()
    cols = lax.broadcasted_iota(jnp.int32, (HEAD, length), 1)
    wanted, copies = [], []
    for i, coded in enumerate(codes):
        head = coded[per * length : per * length + HEAD].astype(jnp.int32)
        for j in range(per):
            k = i * per + j
            place = jnp.max(jnp.where(cols == per + j, head, 0))
            wanted.append(place > 0)
            target = jnp.maximum(place - 1, 0)
            copies.append(pltpu.make_async_copy(room.at[k], surfaces.at[target], sems.at[k]))
    for i, coded in enumerate(codes):
        for j in range(per):
            k = i * per + j

            @pl.when(wanted[k])
            def _():
                head = coded[per * length : per * length + HEAD].astype(jnp.int32)
                step = jnp.where(cols == j, head, -(1 << 15))[:1].astype(jnp.float32)
                scale = jnp.exp2(jnp.max(step, axis=1, keepdims=True) * (1.0 / STEPS))
                value = coded[j * length : (j + 1) * length].astype(jnp.int32).astype(jnp.float32)
                room[k] = value * jnp.abs(value) * (scale * (1.0 / (TOP * TOP)))
                copies[k].start()

    for k in range(total):

        @pl.when(wanted[k])
        def _():
            copies[k].wait()


def settle_peaks_kernel(tiles, per, count, before, *refs):
    codes, table, home_peaks = refs[:count], refs[count], refs[count + 1 : count + 1 + tiles]
    surfaces, peaks, token, room, sems = refs[-5:]
    settle_kernel(per, count, False, before, *codes, surfaces, token, room, sems)
    head = codes[-1][per * surfaces.shape[-1] : per * surfaces.shape[-1] + HEAD].astype(jnp.int32)
    back_peaks = [guest_peak(head, per, j) for j in range(per)]
    for k in range(peaks.shape[0]):
        peaks[k] = 0.0
    for d in range(tiles):
        for j in range(per):
            lane = d * per + j
            slot = table[4, lane]
            peak = home_peaks[d][j]
            if d == 1:
                peak = jnp.where(table[0, lane] == 0, back_peaks[j], peak)

            @pl.when(slot >= 0)
            def _():
                peaks[slot] = peak


def params():
    return pltpu.CompilerParams(vmem_limit_bytes=LIMIT)


def cost(flops=1):
    return pl.CostEstimate(flops=flops, bytes_accessed=1, transcendentals=0)


def body(patches, pair_lists, move_plan):
    own = patches[0, 0]
    length = own.shape[-1]
    slots = pair_lists.shape[-1]
    tiles = lax.axis_size("tile")
    per = (slots + tiles - 1) // tiles
    up_one = tiles - 1
    far = sorted(range(2, up_one), key=lambda d: -min(d, tiles - d))
    groups_below = [far + [up_one], [0]]
    groups_later = [far, [1], [up_one], [0]]

    def lanes_at(d):
        return [d * per + j for j in range(per)]

    def call(kernel, name, outs, *operands, last=(), flops=SETTLE):
        return pl.pallas_call(
            kernel,
            out_shape=outs,
            in_specs=[VMEM if o.dtype in (own.dtype, jnp.int16) else SMEM for o in operands]
            + [ANY] * len(last),
            out_specs=jax.tree.map(lambda o: SMEM if len(o.shape) == 1 or o.dtype == jnp.int32 else VMEM, outs),
            compiler_params=params(),
            cost_estimate=cost(flops),
            name=name,
        )(*operands, *last)

    def picked(name, token, wanted, *arrived):
        lists = [[(f, lane) for d in ds for lane in lanes_at(d)] for _, f, ds in wanted]
        outs = tuple(SDS((len(w), length, length), own.dtype) for w in lists)
        tables = [t for t, _, _ in wanted]
        *sent, token = call(
            functools.partial(gather_kernel, lists),
            name,
            outs + (SDS(token.shape, token.dtype),),
            token,
            *tables,
            own,
            last=arrived,
        )
        return sent, token

    table = pl.pallas_call(
        functools.partial(lanes_kernel, tiles, per),
        out_shape=SDS((5, tiles * per), jnp.int32),
        in_specs=[SMEM, SMEM],
        out_specs=SMEM,
        cost_estimate=cost(LANES),
        name="lanes",
    )(pair_lists, move_plan)
    table_above = shifted(table, "tile", 1)
    (below_0,), same_table = picked("gather_below", table, [(table_above, 2, groups_below[0])])
    below_0 = shifted(below_0, "tile", -1)
    table_before = shifted(same_table, "sect", 1)
    (first_up, below_1, later_0), token = picked(
        "gather_later",
        table,
        [(table, 1, [1]), (table_above, 2, groups_below[1]), (table_before, 2, groups_later[0])],
    )
    up, later_0 = shifted(first_up, "tile", 1), shifted(later_0, "sect", -1)
    below = [below_0, shifted(below_1, "tile", -1)]
    (later_1, later_2), token = picked(
        "gather_next", token, [(table_before, 2, g) for g in groups_later[1:3]], later_0
    )
    later = [later_0, shifted(later_1, "sect", -1), shifted(later_2, "sect", -1)]

    high, low = packed_table(length)
    tables = [jnp.asarray(t) for t in (high, low, high.T.copy(), low.T.copy())]
    result = (SDS((per * length + HEAD, length), jnp.int16), SDS((per,), jnp.float32))

    longer = (SDS((per * length + 2 * HEAD, length), jnp.int16), result[1])
    works = slots // 2
    surfaces_kind, token_kind = SDS((works, length, length), jnp.float32), SDS((1,), jnp.float32)
    peaks_kind = SDS((slots,), jnp.float32)

    def settled(name, all_codes, before, surfaces=None, table=None, home_peaks=()):
        count = len(all_codes)
        extra = ([] if table is None else [table]) + list(home_peaks)
        blank = surfaces is None
        kernel = functools.partial(settle_kernel, per, count, blank)
        if extra:
            kernel = functools.partial(settle_peaks_kernel, tiles, per, count)
        return pl.pallas_call(
            kernel,
            out_shape=(surfaces_kind,) + ((peaks_kind,) if extra else ()) + (token_kind,),
            in_specs=[SMEM] + [VMEM] * count + [SMEM] * len(extra) + ([] if blank else [ANY]),
            out_specs=(ANY,) + ((SMEM,) if extra else ()) + (SMEM,),
            scratch_shapes=[
                pltpu.VMEM((count * per + 1, length, length), jnp.float32),
                pltpu.SemaphoreType.DMA((count * per + works,)),
            ],
            input_output_aliases={} if blank else {1 + count + len(extra): 0},
            compiler_params=params(),
            cost_estimate=cost(SETTLE),
            name=name,
        )(before, *all_codes, *extra, *([] if blank else [surfaces]))

    home_peaks, moving = [None] * tiles, {}

    def paired(d, before, guests, last=(), flops=SETTLE):
        near = [i for i, g in enumerate(groups_below) if d in g or d == 1][0]
        late = [i for i, g in enumerate(groups_later) if d in g][0]
        lane_codes, home_peaks[d] = call(
            functools.partial(
                pair_kernel,
                lanes_at(d),
                0 if d == 1 else groups_below[near].index(d) * per,
                groups_later[late].index(d) * per,
                1 if d == 1 else None,
                d == up_one,
            ),
            f"pairs_{d}",
            longer if d == 1 else result,
            table,
            before,
            own,
            guests,
            below[near],
            later[late],
            *tables,
            last=last,
            flops=flops,
        )
        moving[d] = lane_codes if d == 0 else rotated(lane_codes, "tile", d)
        return home_peaks[d]

    for d in far:
        token = paired(d, token, token, flops=FIRST)
    (later_3,), _ = picked("gather_home", token, [(table_before, 2, groups_later[3])])
    later.append(shifted(later_3, "sect", -1))
    visit_codes, guests = call(
        functools.partial(visit_kernel, lanes_at(1)),
        "visit",
        result,
        table_above,
        token,
        own,
        up,
        *tables,
        last=[below[1]],
    )
    surfaces, before = settled("settle_visit", [visit_codes], guests)
    before = paired(1, before, before)
    before = paired(up_one, before, guests)
    before = paired(0, before, before)
    early = [moving[d] for d in [0] + far]
    surfaces, before = settled("settle_early", early, before, surfaces)
    last = [moving[1], moving[up_one]]
    surfaces, peaks, _ = settled("settle_last", last, before, surfaces, table, home_peaks)
    return surfaces[None, None], peaks[None, None]


def solution(mesh):
    in_specs = (
        P(("groups", "sect"), "tile", "half", None, None),
        P(None, ("groups", "sect"), "tile", "half"),
        P(None, ("groups", "sect"), "tile", "half"),
    )
    out_specs = (
        P(("groups", "sect"), "tile", "half", None, None),
        P(("groups", "sect"), "tile", "half"),
    )
    return jax.shard_map(body, mesh=mesh, in_specs=in_specs, out_specs=out_specs, check_vma=False)
```

```python
import functools

import jax
import jax.numpy as jnp
import ml_dtypes
import numpy as np
from jax import lax
from jax.experimental import pallas as pl
from jax.experimental.pallas import tpu as pltpu
from jax.sharding import PartitionSpec as P

FLOOR = 0.05
TOP = 32700.0
STEPS = 8.0
HEAD = 16
LANES = 4_000_000_000
FIRST = 35_000_000_000
SETTLE = 200_000_000
HALF = 16384.0
TINY = 1e-28
LIMIT = 48 * 1024 * 1024

ANY = pl.BlockSpec(memory_space=pl.ANY)
SMEM = pl.BlockSpec(memory_space=pltpu.SMEM)
VMEM = pl.BlockSpec(memory_space=pltpu.VMEM)
SDS = jax.ShapeDtypeStruct


def shifted(value, axis, steps):
    count = lax.axis_size(axis)
    pairs = [(i, i + steps) for i in range(count) if 0 <= i + steps < count]
    return lax.ppermute(value, axis, pairs)


def rotated(value, axis, steps):
    count = lax.axis_size(axis)
    return lax.ppermute(value, axis, [(i, (i + steps) % count) for i in range(count)])


def packed_table(length):
    half = length // 2
    n = np.arange(length)[:, None]
    v = np.arange(half + 1)[None, :]
    angle = 2.0 * np.pi * ((n * v) % length) / length
    table = np.concatenate([np.cos(angle), np.sin(angle[:, 1:half])], axis=1)
    high = table.astype(np.float32).astype(ml_dtypes.bfloat16)
    low = (table - high.astype(np.float64)).astype(np.float32).astype(ml_dtypes.bfloat16)
    return high, low


def dot(left, right):
    return jnp.dot(left, right, preferred_element_type=jnp.float32)


def pieces(value):
    high = value.astype(jnp.bfloat16)
    low = (value - high.astype(jnp.float32)).astype(jnp.bfloat16)
    return high, low


def two_lines(packed, half, row, col, edge):
    cp, cq = packed[:half, :half], packed[:half, half:]
    sp, sq = packed[half:, :half], packed[half:, half:]
    sq_in = jnp.where(edge, 0.0, sq)
    re1 = cp - sq_in
    im1 = -(jnp.where(row, 0.0, sp) + jnp.where(col, 0.0, cq))
    re2 = jnp.where(row, sp, jnp.where(col, cq, cp + sq))
    im2 = jnp.where(edge, -sq, sp - cq)
    return re1, im1, re2, im2


def normalized_packed(one, two, length):
    half = length // 2
    floor = FLOOR * length * length
    rows = lax.broadcasted_iota(jnp.int32, (half, half), 0)
    cols = lax.broadcasted_iota(jnp.int32, (half, half), 1)
    row, col = rows == 0, cols == 0
    edge, corner = row | col, row & col
    a_re1, a_im1, a_re2, a_im2 = two_lines(one, half, row, col, edge)
    b_re1, b_im1, b_re2, b_im2 = two_lines(two, half, row, col, edge)

    def scaled(a_re, a_im, b_re, b_im):
        re = a_re * b_re + a_im * b_im
        im = a_im * b_re - a_re * b_im
        factor = jnp.minimum(lax.rsqrt(re * re + im * im), 1.0 / floor)
        return re * factor, im * factor

    n_re1, n_im1 = scaled(a_re1, a_im1, b_re1, b_im1)
    n_re2, n_im2 = scaled(a_re2, a_im2, b_re2, b_im2)

    def real_corner(value, start_row, start_col):
        a = one[start_row : start_row + half, start_col : start_col + half]
        b = two[start_row : start_row + half, start_col : start_col + half]
        product = a * b
        alone = 0.5 * product / jnp.maximum(jnp.abs(product), floor)
        return jnp.where(corner, alone, value)

    cp = jnp.where(edge, n_re1, n_re1 + n_re2)
    cq = jnp.where(row, -n_im1, jnp.where(col, n_re2, -(n_im1 + n_im2)))
    sp = jnp.where(row, n_re2, jnp.where(col, -n_im1, n_im2 - n_im1))
    sq = jnp.where(edge, -n_im2, n_re2 - n_re1)
    cp = real_corner(cp, 0, 0)
    cq = real_corner(cq, 0, half)
    sp = real_corner(sp, half, 0)
    sq = real_corner(sq, half, half)
    packed = jnp.concatenate(
        [jnp.concatenate([cp, cq], axis=1), jnp.concatenate([sp, sq], axis=1)], axis=0
    )
    return packed * (2.0 / length)


def lanes_kernel(tiles, per, pairs, plan, table):
    slots = pairs.shape[-1]
    me = lax.axis_index("tile")
    for lane in range(tiles * per):
        table[0, lane] = -1
        for field in range(1, 3):
            table[field, lane] = 0
        for field in range(3, 5):
            table[field, lane] = -1
    targets = [plan[0, 0, 0, k] for k in range(slots)]
    for k, target in enumerate(targets):
        rank = jnp.int32(0)
        for earlier in targets[:k]:
            rank += (earlier == target).astype(jnp.int32)
        distance = lax.rem(target - me + tiles, tiles)
        lane = distance * per + rank

        @pl.when(target >= 0)
        def _():
            for field in range(3):
                table[field, lane] = pairs[field, 0, 0, k]
            table[3, lane] = plan[1, 0, 0, k]
            table[4, lane] = k


def gather_kernel(lanes_of, *refs):
    count = len(lanes_of)
    tables, patches = refs[1 : count + 1], refs[count + 1]
    *sent, token = refs[-count - 1 :]
    for at in np.ndindex(*token.shape):
        token[at] = refs[0][at]
    for table, wanted, out in zip(tables, lanes_of, sent):
        for i, (field, lane) in enumerate(wanted):
            out[i] = patches[table[field, lane]]


def correlate(firsts, seconds, places, guests, th, tl, sh, sl, codes, peaks):
    length = codes.shape[-1]
    per = len(firsts)
    packed = [dot(p, th[...]) + dot(p, tl[...]) for p in firsts + seconds]
    packed = [pieces(p) for p in packed]
    packed = [dot(sh[...], h) + dot(sh[...], w) + dot(sl[...], h) for h, w in packed]
    both = [normalized_packed(packed[j], packed[per + j], length) for j in range(per)]
    both = [pieces(p) for p in both]
    both = [dot(th[...], h) + dot(th[...], w) + dot(tl[...], h) for h, w in both]
    both = [pieces(p) for p in both]
    both = [dot(h, sh[...]) + dot(h, sl[...]) + dot(w, sh[...]) for h, w in both]
    cols = lax.broadcasted_iota(jnp.int32, (HEAD, length), 1)
    head = guest_head(guests, length)
    for j, surface in enumerate(both):
        peaks[j] = jnp.max(surface)
        size = jnp.max(jnp.max(jnp.abs(surface), axis=0, keepdims=True), axis=1, keepdims=True)
        step = jnp.ceil(STEPS * jnp.log2(jnp.maximum(size, TINY)))
        grown = jnp.abs(surface) * (TOP * TOP * jnp.exp2(step * (-1.0 / STEPS)))
        root = grown * lax.rsqrt(jnp.maximum(grown, TINY))
        whole = (root + 0.5).astype(jnp.int32)
        whole = jnp.where(surface < 0, -whole, whole)
        codes[j * length : (j + 1) * length] = whole.astype(jnp.int16)
        head = jnp.where(cols == j, step.astype(jnp.int32), head)
        head = jnp.where(cols == per + j, places[j], head)
    codes[per * length : per * length + HEAD] = head.astype(jnp.int16)


def guest_head(guests, length):
    cols = lax.broadcasted_iota(jnp.int32, (HEAD, length), 1)
    head = jnp.zeros((HEAD, length), jnp.int32)
    if guests is None:
        return head
    per = guests.shape[0]
    for j in range(per):
        peak = jnp.full((HEAD, length), guests[j])
        power = jnp.ceil(jnp.log2(jnp.maximum(jnp.abs(peak), TINY)))
        share = peak * jnp.exp2(-power) * HALF
        high = share.astype(jnp.int32)
        low = ((share - high.astype(jnp.float32)) * HALF).astype(jnp.int32)
        for i, part in enumerate((power.astype(jnp.int32), high, low)):
            head = jnp.where(cols == 2 * per + 3 * j + i, part, head)
    return head


def guest_peak(head, per, j):
    cols = lax.broadcasted_iota(jnp.int32, head.shape, 1)

    def part(i):
        one = jnp.where(cols == 2 * per + 3 * j + i, head, 0)[:1]
        return jnp.sum(one.astype(jnp.float32), axis=1, keepdims=True)

    return jnp.max((part(1) + part(2) * (1.0 / HALF)) * (1.0 / HALF) * jnp.exp2(part(0)))


def any_of(flags):
    some = flags[0]
    for flag in flags[1:]:
        some = some | flag
    return some


def pair_kernel(lanes, at_below, at_later, live_kind, with_guests, table, before, own, *refs):
    per = len(lanes)
    at_hand = refs[1:3]
    guests = refs[0] if with_guests else None
    th, tl, sh, sl = refs[3:7]
    codes, peaks = refs[-2:]
    kinds = [table[0, lane] for lane in lanes]
    for j in range(per):
        peaks[j] = 0.0
    codes[per * codes.shape[-1] : per * codes.shape[-1] + HEAD] = guest_head(guests, codes.shape[-1]).astype(jnp.int16)
    wanted = [k >= 0 if live_kind is None else k == live_kind for k in kinds]

    @pl.when(any_of(wanted))
    def _():
        places = [jnp.where(w, table[3, lane] + 1, 0) for w, lane in zip(wanted, lanes)]
        firsts = [own[table[1, lane]] for lane in lanes]
        seconds = [at_hand[1][at_later + j] for j in range(per)]
        if live_kind is None:
            seconds = [
                jnp.where(kinds[j] == 0, at_hand[0][at_below + j], seconds[j]) for j in range(per)
            ]
        correlate(firsts, seconds, places, guests, th, tl, sh, sl, codes, peaks)


def pair_send_kernel(pair, wanted, table, before, own, guests, below, later, th, tl, sh, sl, other, *refs):
    *_, codes, peaks, sent = refs
    for i, (field, lane) in enumerate(wanted):
        sent[i] = own[other[field, lane]]
    pair(table, before, own, guests, below, later, th, tl, sh, sl, codes, peaks)


def visit_kernel(lanes, table_above, token, own, up, th, tl, sh, sl, _, codes, peaks):
    per = len(lanes)
    length = codes.shape[-1]
    row = lax.axis_index("tile")
    for j in range(per):
        peaks[j] = 0.0
    codes[per * length : per * length + HEAD] = jnp.zeros((HEAD, length), jnp.int32).astype(jnp.int16)
    kinds = [table_above[0, lane] for lane in lanes]

    @pl.when((row > 0) & any_of([kind == 0 for kind in kinds]))
    def _():
        firsts = [up[j] for j in range(per)]
        seconds = [own[table_above[2, lane]] for lane in lanes]
        places = [
            jnp.where(kind == 0, table_above[3, lane] + 1, 0) for kind, lane in zip(kinds, lanes)
        ]
        correlate(firsts, seconds, places, None, th, tl, sh, sl, codes, peaks)


def settle_kernel(per, count, blank, before, *refs):
    codes = refs[:count]
    surfaces, token, room, sems = refs[-4:]
    length = surfaces.shape[-1]
    total = count * per
    token[0] = 0.0
    if blank:
        room[total] = jnp.zeros((length, length), jnp.float32)
        fills = [
            pltpu.make_async_copy(room.at[total], surfaces.at[k], sems.at[total + k])
            for k in range(surfaces.shape[0])
        ]
        for fill in fills:
            fill.start()
        for fill in fills:
            fill.wait()
    cols = lax.broadcasted_iota(jnp.int32, (HEAD, length), 1)
    wanted, copies = [], []
    for i, coded in enumerate(codes):
        head = coded[per * length : per * length + HEAD].astype(jnp.int32)
        for j in range(per):
            k = i * per + j
            place = jnp.max(jnp.where(cols == per + j, head, 0))
            wanted.append(place > 0)
            target = jnp.maximum(place - 1, 0)
            copies.append(pltpu.make_async_copy(room.at[k], surfaces.at[target], sems.at[k]))
    for i, coded in enumerate(codes):
        for j in range(per):
            k = i * per + j

            @pl.when(wanted[k])
            def _():
                head = coded[per * length : per * length + HEAD].astype(jnp.int32)
                step = jnp.where(cols == j, head, -(1 << 15))[:1].astype(jnp.float32)
                scale = jnp.exp2(jnp.max(step, axis=1, keepdims=True) * (1.0 / STEPS))
                value = coded[j * length : (j + 1) * length].astype(jnp.int32).astype(jnp.float32)
                room[k] = value * jnp.abs(value) * (scale * (1.0 / (TOP * TOP)))
                copies[k].start()

    for k in range(total):

        @pl.when(wanted[k])
        def _():
            copies[k].wait()


def settle_peaks_kernel(tiles, per, count, before, *refs):
    codes, table, home_peaks = refs[:count], refs[count], refs[count + 1 : count + 1 + tiles]
    surfaces, peaks, token, room, sems = refs[-5:]
    settle_kernel(per, count, False, before, *codes, surfaces, token, room, sems)
    head = codes[-1][per * surfaces.shape[-1] : per * surfaces.shape[-1] + HEAD].astype(jnp.int32)
    back_peaks = [guest_peak(head, per, j) for j in range(per)]
    for k in range(peaks.shape[0]):
        peaks[k] = 0.0
    for d in range(tiles):
        for j in range(per):
            lane = d * per + j
            slot = table[4, lane]
            peak = home_peaks[d][j]
            if d == 1:
                peak = jnp.where(table[0, lane] == 0, back_peaks[j], peak)

            @pl.when(slot >= 0)
            def _():
                peaks[slot] = peak


def params():
    return pltpu.CompilerParams(vmem_limit_bytes=LIMIT)


def cost(flops=1):
    return pl.CostEstimate(flops=flops, bytes_accessed=1, transcendentals=0)


def body(patches, pair_lists, move_plan):
    own = patches[0, 0]
    length = own.shape[-1]
    slots = pair_lists.shape[-1]
    tiles = lax.axis_size("tile")
    per = (slots + tiles - 1) // tiles
    up_one = tiles - 1
    far = sorted(range(2, up_one), key=lambda d: -min(d, tiles - d))
    groups_below = [far + [up_one], [0]]
    groups_later = [far, [1], [up_one], [0]]

    def lanes_at(d):
        return [d * per + j for j in range(per)]

    def call(kernel, name, outs, *operands, last=(), flops=SETTLE):
        return pl.pallas_call(
            kernel,
            out_shape=outs,
            in_specs=[VMEM if o.dtype in (own.dtype, jnp.int16) else SMEM for o in operands]
            + [ANY] * len(last),
            out_specs=jax.tree.map(lambda o: SMEM if len(o.shape) == 1 or o.dtype == jnp.int32 else VMEM, outs),
            compiler_params=params(),
            cost_estimate=cost(flops),
            name=name,
        )(*operands, *last)

    def picked(name, token, wanted, *arrived):
        lists = [[(f, lane) for d in ds for lane in lanes_at(d)] for _, f, ds in wanted]
        outs = tuple(SDS((len(w), length, length), own.dtype) for w in lists)
        tables = [t for t, _, _ in wanted]
        *sent, token = call(
            functools.partial(gather_kernel, lists),
            name,
            outs + (SDS(token.shape, token.dtype),),
            token,
            *tables,
            own,
            last=arrived,
        )
        return sent, token

    table = pl.pallas_call(
        functools.partial(lanes_kernel, tiles, per),
        out_shape=SDS((5, tiles * per), jnp.int32),
        in_specs=[SMEM, SMEM],
        out_specs=SMEM,
        cost_estimate=cost(LANES),
        name="lanes",
    )(pair_lists, move_plan)
    table_above = shifted(table, "tile", 1)
    (below_0,), same_table = picked("gather_below", table, [(table_above, 2, groups_below[0])])
    below_0 = shifted(below_0, "tile", -1)
    table_before = shifted(same_table, "sect", 1)
    (first_up, below_1, later_0), token = picked(
        "gather_later",
        table,
        [(table, 1, [1]), (table_above, 2, groups_below[1]), (table_before, 2, groups_later[0])],
    )
    up, later_0 = shifted(first_up, "tile", 1), shifted(later_0, "sect", -1)
    below = [below_0, shifted(below_1, "tile", -1)]
    (later_1, later_2), token = picked(
        "gather_next", token, [(table_before, 2, g) for g in groups_later[1:3]], later_0
    )
    later = [later_0, shifted(later_1, "sect", -1), shifted(later_2, "sect", -1)]

    high, low = packed_table(length)
    tables = [jnp.asarray(t) for t in (high, low, high.T.copy(), low.T.copy())]
    result = (SDS((per * length + HEAD, length), jnp.int16), SDS((per,), jnp.float32))

    longer = (SDS((per * length + 2 * HEAD, length), jnp.int16), result[1])
    works = slots // 2
    surfaces_kind, token_kind = SDS((works, length, length), jnp.float32), SDS((1,), jnp.float32)
    peaks_kind = SDS((slots,), jnp.float32)

    def settled(name, all_codes, before, surfaces=None, table=None, home_peaks=()):
        count = len(all_codes)
        extra = ([] if table is None else [table]) + list(home_peaks)
        blank = surfaces is None
        kernel = functools.partial(settle_kernel, per, count, blank)
        if extra:
            kernel = functools.partial(settle_peaks_kernel, tiles, per, count)
        return pl.pallas_call(
            kernel,
            out_shape=(surfaces_kind,) + ((peaks_kind,) if extra else ()) + (token_kind,),
            in_specs=[SMEM] + [VMEM] * count + [SMEM] * len(extra) + ([] if blank else [ANY]),
            out_specs=(ANY,) + ((SMEM,) if extra else ()) + (SMEM,),
            scratch_shapes=[
                pltpu.VMEM((count * per + 1, length, length), jnp.float32),
                pltpu.SemaphoreType.DMA((count * per + works,)),
            ],
            input_output_aliases={} if blank else {1 + count + len(extra): 0},
            compiler_params=params(),
            cost_estimate=cost(SETTLE),
            name=name,
        )(before, *all_codes, *extra, *([] if blank else [surfaces]))

    home_peaks, moving = [None] * tiles, {}

    def paired(d, before, guests, last=(), flops=SETTLE, send=()):
        near = [i for i, g in enumerate(groups_below) if d in g or d == 1][0]
        late = [i for i, g in enumerate(groups_later) if d in g][0]
        kernel = functools.partial(
            pair_kernel,
            lanes_at(d),
            0 if d == 1 else groups_below[near].index(d) * per,
            groups_later[late].index(d) * per,
            1 if d == 1 else None,
            d == up_one,
        )
        outs = longer if d == 1 else result
        if send:
            wanted = [(2, lane) for e in send for lane in lanes_at(e)]
            kernel = functools.partial(pair_send_kernel, kernel, wanted)
            outs += (SDS((len(wanted), length, length), own.dtype),)
        lane_codes, home_peaks[d], *sent = call(
            kernel,
            f"pairs_{d}",
            outs,
            table,
            before,
            own,
            guests,
            below[near],
            later[late],
            *tables,
            *([table_before] if send else []),
            last=last,
            flops=flops,
        )
        moving[d] = lane_codes if d == 0 else rotated(lane_codes, "tile", d)
        return home_peaks[d], sent

    for d in far:
        send = groups_later[3] if d == far[-1] else ()
        token, sent = paired(d, token, token, flops=FIRST, send=send)
    later.append(shifted(sent[0], "sect", -1))
    visit_codes, guests = call(
        functools.partial(visit_kernel, lanes_at(1)),
        "visit",
        result,
        table_above,
        token,
        own,
        up,
        *tables,
        last=[below[1]],
    )
    surfaces, before = settled("settle_visit", [visit_codes], guests)
    before, _ = paired(1, before, before)
    before, _ = paired(up_one, before, guests)
    before, _ = paired(0, before, before)
    early = [moving[d] for d in [0] + far]
    surfaces, before = settled("settle_early", early, before, surfaces)
    last = [moving[1], moving[up_one]]
    surfaces, peaks, _ = settled("settle_last", last, before, surfaces, table, home_peaks)
    return surfaces[None, None], peaks[None, None]


def solution(mesh):
    in_specs = (
        P(("groups", "sect"), "tile", "half", None, None),
        P(None, ("groups", "sect"), "tile", "half"),
        P(None, ("groups", "sect"), "tile", "half"),
    )
    out_specs = (
        P(("groups", "sect"), "tile", "half", None, None),
        P(("groups", "sect"), "tile", "half"),
    )
    return jax.shard_map(body, mesh=mesh, in_specs=in_specs, out_specs=out_specs, check_vma=False)
```

```python
import functools

import jax
import jax.numpy as jnp
import ml_dtypes
import numpy as np
from jax import lax
from jax.experimental import pallas as pl
from jax.experimental.pallas import tpu as pltpu
from jax.sharding import PartitionSpec as P

FLOOR = 0.05
TOP = 32700.0
STEPS = 8.0
HEAD = 16
LANES = 4_000_000_000
FIRST = 35_000_000_000
SETTLE = 200_000_000
HALF = 16384.0
TINY = 1e-28
LIMIT = 48 * 1024 * 1024

ANY = pl.BlockSpec(memory_space=pl.ANY)
SMEM = pl.BlockSpec(memory_space=pltpu.SMEM)
VMEM = pl.BlockSpec(memory_space=pltpu.VMEM)
SDS = jax.ShapeDtypeStruct


def shifted(value, axis, steps):
    count = lax.axis_size(axis)
    pairs = [(i, i + steps) for i in range(count) if 0 <= i + steps < count]
    return lax.ppermute(value, axis, pairs)


def rotated(value, axis, steps):
    count = lax.axis_size(axis)
    return lax.ppermute(value, axis, [(i, (i + steps) % count) for i in range(count)])


def packed_table(length):
    half = length // 2
    n = np.arange(length)[:, None]
    v = np.arange(half + 1)[None, :]
    angle = 2.0 * np.pi * ((n * v) % length) / length
    table = np.concatenate([np.cos(angle), np.sin(angle[:, 1:half])], axis=1)
    high = table.astype(np.float32).astype(ml_dtypes.bfloat16)
    low = (table - high.astype(np.float64)).astype(np.float32).astype(ml_dtypes.bfloat16)
    return high, low


def dot(left, right):
    return jnp.dot(left, right, preferred_element_type=jnp.float32)


def pieces(value):
    high = value.astype(jnp.bfloat16)
    low = (value - high.astype(jnp.float32)).astype(jnp.bfloat16)
    return high, low


def two_lines(packed, half, row, col, edge):
    cp, cq = packed[:half, :half], packed[:half, half:]
    sp, sq = packed[half:, :half], packed[half:, half:]
    sq_in = jnp.where(edge, 0.0, sq)
    re1 = cp - sq_in
    im1 = -(jnp.where(row, 0.0, sp) + jnp.where(col, 0.0, cq))
    re2 = jnp.where(row, sp, jnp.where(col, cq, cp + sq))
    im2 = jnp.where(edge, -sq, sp - cq)
    return re1, im1, re2, im2


def normalized_packed(one, two, length):
    half = length // 2
    floor = FLOOR * length * length
    rows = lax.broadcasted_iota(jnp.int32, (half, half), 0)
    cols = lax.broadcasted_iota(jnp.int32, (half, half), 1)
    row, col = rows == 0, cols == 0
    edge, corner = row | col, row & col
    a_re1, a_im1, a_re2, a_im2 = two_lines(one, half, row, col, edge)
    b_re1, b_im1, b_re2, b_im2 = two_lines(two, half, row, col, edge)

    def scaled(a_re, a_im, b_re, b_im):
        re = a_re * b_re + a_im * b_im
        im = a_im * b_re - a_re * b_im
        factor = jnp.minimum(lax.rsqrt(re * re + im * im), 1.0 / floor)
        return re * factor, im * factor

    n_re1, n_im1 = scaled(a_re1, a_im1, b_re1, b_im1)
    n_re2, n_im2 = scaled(a_re2, a_im2, b_re2, b_im2)

    def real_corner(value, start_row, start_col):
        a = one[start_row : start_row + half, start_col : start_col + half]
        b = two[start_row : start_row + half, start_col : start_col + half]
        product = a * b
        alone = 0.5 * product / jnp.maximum(jnp.abs(product), floor)
        return jnp.where(corner, alone, value)

    cp = jnp.where(edge, n_re1, n_re1 + n_re2)
    cq = jnp.where(row, -n_im1, jnp.where(col, n_re2, -(n_im1 + n_im2)))
    sp = jnp.where(row, n_re2, jnp.where(col, -n_im1, n_im2 - n_im1))
    sq = jnp.where(edge, -n_im2, n_re2 - n_re1)
    cp = real_corner(cp, 0, 0)
    cq = real_corner(cq, 0, half)
    sp = real_corner(sp, half, 0)
    sq = real_corner(sq, half, half)
    packed = jnp.concatenate(
        [jnp.concatenate([cp, cq], axis=1), jnp.concatenate([sp, sq], axis=1)], axis=0
    )
    return packed * (2.0 / length)


def lanes_kernel(tiles, per, pairs, plan, table):
    slots = pairs.shape[-1]
    me = lax.axis_index("tile")
    for lane in range(tiles * per):
        table[0, lane] = -1
        for field in range(1, 3):
            table[field, lane] = 0
        for field in range(3, 5):
            table[field, lane] = -1
    targets = [plan[0, 0, 0, k] for k in range(slots)]
    for k, target in enumerate(targets):
        rank = jnp.int32(0)
        for earlier in targets[:k]:
            rank += (earlier == target).astype(jnp.int32)
        distance = lax.rem(target - me + tiles, tiles)
        lane = distance * per + rank

        @pl.when(target >= 0)
        def _():
            for field in range(3):
                table[field, lane] = pairs[field, 0, 0, k]
            table[3, lane] = plan[1, 0, 0, k]
            table[4, lane] = k


def gather_kernel(lanes_of, *refs):
    count = len(lanes_of)
    tables, patches = refs[1 : count + 1], refs[count + 1]
    *sent, token = refs[-count - 1 :]
    for at in np.ndindex(*token.shape):
        token[at] = refs[0][at]
    for table, wanted, out in zip(tables, lanes_of, sent):
        for i, (field, lane) in enumerate(wanted):
            out[i] = patches[table[field, lane]]


def correlate(firsts, seconds, places, guests, th, tl, sh, sl, codes, peaks):
    length = codes.shape[-1]
    per = len(firsts)
    packed = [dot(p, th[...]) + dot(p, tl[...]) for p in firsts + seconds]
    packed = [pieces(p) for p in packed]
    packed = [dot(sh[...], h) + dot(sh[...], w) + dot(sl[...], h) for h, w in packed]
    both = [normalized_packed(packed[j], packed[per + j], length) for j in range(per)]
    both = [pieces(p) for p in both]
    both = [dot(th[...], h) + dot(th[...], w) + dot(tl[...], h) for h, w in both]
    both = [pieces(p) for p in both]
    both = [dot(h, sh[...]) + dot(h, sl[...]) + dot(w, sh[...]) for h, w in both]
    cols = lax.broadcasted_iota(jnp.int32, (HEAD, length), 1)
    head = guest_head(guests, length)
    for j, surface in enumerate(both):
        peaks[j] = jnp.max(surface)
        size = jnp.max(jnp.max(jnp.abs(surface), axis=0, keepdims=True), axis=1, keepdims=True)
        step = jnp.ceil(STEPS * jnp.log2(jnp.maximum(size, TINY)))
        grown = jnp.abs(surface) * (TOP * TOP * jnp.exp2(step * (-1.0 / STEPS)))
        root = grown * lax.rsqrt(jnp.maximum(grown, TINY))
        whole = (root + 0.5).astype(jnp.int32)
        whole = jnp.where(surface < 0, -whole, whole)
        codes[j * length : (j + 1) * length] = whole.astype(jnp.int16)
        head = jnp.where(cols == j, step.astype(jnp.int32), head)
        head = jnp.where(cols == per + j, places[j], head)
    codes[per * length : per * length + HEAD] = head.astype(jnp.int16)


def guest_head(guests, length):
    cols = lax.broadcasted_iota(jnp.int32, (HEAD, length), 1)
    head = jnp.zeros((HEAD, length), jnp.int32)
    if guests is None:
        return head
    per = guests.shape[0]
    for j in range(per):
        peak = jnp.full((HEAD, length), guests[j])
        power = jnp.ceil(jnp.log2(jnp.maximum(jnp.abs(peak), TINY)))
        share = peak * jnp.exp2(-power) * HALF
        high = share.astype(jnp.int32)
        low = ((share - high.astype(jnp.float32)) * HALF).astype(jnp.int32)
        for i, part in enumerate((power.astype(jnp.int32), high, low)):
            head = jnp.where(cols == 2 * per + 3 * j + i, part, head)
    return head


def guest_peak(head, per, j):
    cols = lax.broadcasted_iota(jnp.int32, head.shape, 1)

    def part(i):
        one = jnp.where(cols == 2 * per + 3 * j + i, head, 0)[:1]
        return jnp.sum(one.astype(jnp.float32), axis=1, keepdims=True)

    return jnp.max((part(1) + part(2) * (1.0 / HALF)) * (1.0 / HALF) * jnp.exp2(part(0)))


def any_of(flags):
    some = flags[0]
    for flag in flags[1:]:
        some = some | flag
    return some


def pair_kernel(lanes, at_below, at_later, live_kind, with_guests, table, before, own, *refs):
    per = len(lanes)
    at_hand = refs[1:3]
    guests = refs[0] if with_guests else None
    th, tl, sh, sl = refs[3:7]
    codes, peaks = refs[-2:]
    kinds = [table[0, lane] for lane in lanes]
    for j in range(per):
        peaks[j] = 0.0
    codes[per * codes.shape[-1] : per * codes.shape[-1] + HEAD] = guest_head(guests, codes.shape[-1]).astype(jnp.int16)
    wanted = [k >= 0 if live_kind is None else k == live_kind for k in kinds]

    @pl.when(any_of(wanted))
    def _():
        places = [jnp.where(w, table[3, lane] + 1, 0) for w, lane in zip(wanted, lanes)]
        firsts = [own[table[1, lane]] for lane in lanes]
        seconds = [at_hand[1][at_later + j] for j in range(per)]
        if live_kind is None:
            seconds = [
                jnp.where(kinds[j] == 0, at_hand[0][at_below + j], seconds[j]) for j in range(per)
            ]
        correlate(firsts, seconds, places, guests, th, tl, sh, sl, codes, peaks)


def pair_send_kernel(pair, wanted, table, before, own, guests, below, later, th, tl, sh, sl, other, *refs):
    *_, codes, peaks, sent = refs
    for i, (field, lane) in enumerate(wanted):
        sent[i] = own[other[field, lane]]
    pair(table, before, own, guests, below, later, th, tl, sh, sl, codes, peaks)


def visit_kernel(lanes, table_above, token, own, up, th, tl, sh, sl, _, codes, peaks):
    per = len(lanes)
    length = codes.shape[-1]
    row = lax.axis_index("tile")
    for j in range(per):
        peaks[j] = 0.0
    codes[per * length : per * length + HEAD] = jnp.zeros((HEAD, length), jnp.int32).astype(jnp.int16)
    kinds = [table_above[0, lane] for lane in lanes]

    @pl.when((row > 0) & any_of([kind == 0 for kind in kinds]))
    def _():
        firsts = [up[j] for j in range(per)]
        seconds = [own[table_above[2, lane]] for lane in lanes]
        places = [
            jnp.where(kind == 0, table_above[3, lane] + 1, 0) for kind, lane in zip(kinds, lanes)
        ]
        correlate(firsts, seconds, places, None, th, tl, sh, sl, codes, peaks)


def settle_kernel(per, count, blank, before, *refs):
    codes = refs[:count]
    surfaces, token, room, sems = refs[-4:]
    length = surfaces.shape[-1]
    total = count * per
    token[0] = 0.0
    if blank:
        room[total] = jnp.zeros((length, length), jnp.float32)
        fills = [
            pltpu.make_async_copy(room.at[total], surfaces.at[k], sems.at[total + k])
            for k in range(surfaces.shape[0])
        ]
        for fill in fills:
            fill.start()
        for fill in fills:
            fill.wait()
    cols = lax.broadcasted_iota(jnp.int32, (HEAD, length), 1)
    wanted, copies = [], []
    for i, coded in enumerate(codes):
        head = coded[per * length : per * length + HEAD].astype(jnp.int32)
        for j in range(per):
            k = i * per + j
            place = jnp.max(jnp.where(cols == per + j, head, 0))
            wanted.append(place > 0)
            target = jnp.maximum(place - 1, 0)
            copies.append(pltpu.make_async_copy(room.at[k], surfaces.at[target], sems.at[k]))
    for i, coded in enumerate(codes):
        for j in range(per):
            k = i * per + j

            @pl.when(wanted[k])
            def _():
                head = coded[per * length : per * length + HEAD].astype(jnp.int32)
                step = jnp.where(cols == j, head, -(1 << 15))[:1].astype(jnp.float32)
                scale = jnp.exp2(jnp.max(step, axis=1, keepdims=True) * (1.0 / STEPS))
                value = coded[j * length : (j + 1) * length].astype(jnp.int32).astype(jnp.float32)
                room[k] = value * jnp.abs(value) * (scale * (1.0 / (TOP * TOP)))
                copies[k].start()

    for k in range(total):

        @pl.when(wanted[k])
        def _():
            copies[k].wait()


def settle_peaks_kernel(tiles, per, count, before, *refs):
    codes, table, home_peaks = refs[:count], refs[count], refs[count + 1 : count + 1 + tiles]
    surfaces, peaks, token, room, sems = refs[-5:]
    settle_kernel(per, count, False, before, *codes, surfaces, token, room, sems)
    head = codes[-1][per * surfaces.shape[-1] : per * surfaces.shape[-1] + HEAD].astype(jnp.int32)
    back_peaks = [guest_peak(head, per, j) for j in range(per)]
    for k in range(peaks.shape[0]):
        peaks[k] = 0.0
    for d in range(tiles):
        for j in range(per):
            lane = d * per + j
            slot = table[4, lane]
            peak = home_peaks[d][j]
            if d == 1:
                peak = jnp.where(table[0, lane] == 0, back_peaks[j], peak)

            @pl.when(slot >= 0)
            def _():
                peaks[slot] = peak


def params():
    return pltpu.CompilerParams(vmem_limit_bytes=LIMIT)


def cost(flops=1):
    return pl.CostEstimate(flops=flops, bytes_accessed=1, transcendentals=0)


def body(patches, pair_lists, move_plan):
    own = patches[0, 0]
    length = own.shape[-1]
    slots = pair_lists.shape[-1]
    tiles = lax.axis_size("tile")
    per = (slots + tiles - 1) // tiles
    up_one = tiles - 1
    far = sorted(range(2, up_one), key=lambda d: -min(d, tiles - d))
    groups_below = [far + [up_one], [0]]
    groups_later = [far, [1], [up_one], [0]]

    def lanes_at(d):
        return [d * per + j for j in range(per)]

    def call(kernel, name, outs, *operands, last=(), flops=SETTLE):
        return pl.pallas_call(
            kernel,
            out_shape=outs,
            in_specs=[VMEM if o.dtype in (own.dtype, jnp.int16) else SMEM for o in operands]
            + [ANY] * len(last),
            out_specs=jax.tree.map(lambda o: SMEM if len(o.shape) == 1 or o.dtype == jnp.int32 else VMEM, outs),
            compiler_params=params(),
            cost_estimate=cost(flops),
            name=name,
        )(*operands, *last)

    def picked(name, token, wanted, *arrived):
        lists = [[(f, lane) for d in ds for lane in lanes_at(d)] for _, f, ds in wanted]
        outs = tuple(SDS((len(w), length, length), own.dtype) for w in lists)
        tables = [t for t, _, _ in wanted]
        *sent, token = call(
            functools.partial(gather_kernel, lists),
            name,
            outs + (SDS(token.shape, token.dtype),),
            token,
            *tables,
            own,
            last=arrived,
        )
        return sent, token

    table = pl.pallas_call(
        functools.partial(lanes_kernel, tiles, per),
        out_shape=SDS((5, tiles * per), jnp.int32),
        in_specs=[SMEM, SMEM],
        out_specs=SMEM,
        cost_estimate=cost(LANES),
        name="lanes",
    )(pair_lists, move_plan)
    table_above = shifted(table, "tile", 1)
    (below_0,), same_table = picked("gather_below", table, [(table_above, 2, groups_below[0])])
    below_0 = shifted(below_0, "tile", -1)
    table_before = shifted(same_table, "sect", 1)
    (first_up, below_1, later_0), token = picked(
        "gather_later",
        table,
        [(table, 1, [1]), (table_above, 2, groups_below[1]), (table_before, 2, groups_later[0])],
    )
    up, later_0 = shifted(first_up, "tile", 1), shifted(later_0, "sect", -1)
    below = [below_0, shifted(below_1, "tile", -1)]
    (later_1, later_2), token = picked(
        "gather_next", token, [(table_before, 2, g) for g in groups_later[1:3]], later_0
    )
    later = [later_0, shifted(later_1, "sect", -1), shifted(later_2, "sect", -1)]

    high, low = packed_table(length)
    tables = [jnp.asarray(t) for t in (high, low, high.T.copy(), low.T.copy())]
    result = (SDS((per * length + HEAD, length), jnp.int16), SDS((per,), jnp.float32))

    longer = (SDS((per * length + 2 * HEAD, length), jnp.int16), result[1])
    works = slots // 2
    surfaces_kind, token_kind = SDS((works, length, length), jnp.float32), SDS((1,), jnp.float32)
    peaks_kind = SDS((slots,), jnp.float32)

    def settled(name, all_codes, before, surfaces=None, table=None, home_peaks=()):
        count = len(all_codes)
        extra = ([] if table is None else [table]) + list(home_peaks)
        blank = surfaces is None
        kernel = functools.partial(settle_kernel, per, count, blank)
        if extra:
            kernel = functools.partial(settle_peaks_kernel, tiles, per, count)
        return pl.pallas_call(
            kernel,
            out_shape=(surfaces_kind,) + ((peaks_kind,) if extra else ()) + (token_kind,),
            in_specs=[SMEM] + [VMEM] * count + [SMEM] * len(extra) + ([] if blank else [ANY]),
            out_specs=(ANY,) + ((SMEM,) if extra else ()) + (SMEM,),
            scratch_shapes=[
                pltpu.VMEM((count * per + 1, length, length), jnp.float32),
                pltpu.SemaphoreType.DMA((count * per + works,)),
            ],
            input_output_aliases={} if blank else {1 + count + len(extra): 0},
            compiler_params=params(),
            cost_estimate=cost(SETTLE),
            name=name,
        )(before, *all_codes, *extra, *([] if blank else [surfaces]))

    home_peaks, moving = [None] * tiles, {}

    def paired(d, before, guests, last=(), flops=SETTLE, send=()):
        near = [i for i, g in enumerate(groups_below) if d in g or d == 1][0]
        late = [i for i, g in enumerate(groups_later) if d in g][0]
        kernel = functools.partial(
            pair_kernel,
            lanes_at(d),
            0 if d == 1 else groups_below[near].index(d) * per,
            groups_later[late].index(d) * per,
            1 if d == 1 else None,
            d == up_one,
        )
        outs = longer if d == 1 else result
        if send:
            wanted = [(2, lane) for e in send for lane in lanes_at(e)]
            kernel = functools.partial(pair_send_kernel, kernel, wanted)
            outs += (SDS((len(wanted), length, length), own.dtype),)
        lane_codes, home_peaks[d], *sent = call(
            kernel,
            f"pairs_{d}",
            outs,
            table,
            before,
            own,
            guests,
            below[near],
            later[late],
            *tables,
            *([table_before] if send else []),
            last=last,
            flops=flops,
        )
        moving[d] = lane_codes if d == 0 else rotated(lane_codes, "tile", d)
        return home_peaks[d], sent

    for d in far:
        send = groups_later[3] if d == far[-1] else ()
        token, sent = paired(d, token, token, flops=FIRST, send=send)
    later.append(shifted(sent[0], "sect", -1))
    visit_codes, guests = call(
        functools.partial(visit_kernel, lanes_at(1)),
        "visit",
        result,
        table_above,
        token,
        own,
        up,
        *tables,
        last=[below[1]],
    )
    before, _ = paired(1, guests, guests)
    before, _ = paired(up_one, before, guests)
    surfaces, before = settled("settle_visit", [visit_codes], before)
    before, _ = paired(0, before, before)
    early = [moving[d] for d in [0] + far]
    surfaces, before = settled("settle_early", early, before, surfaces)
    last = [moving[1], moving[up_one]]
    surfaces, peaks, _ = settled("settle_last", last, before, surfaces, table, home_peaks)
    return surfaces[None, None], peaks[None, None]


def solution(mesh):
    in_specs = (
        P(("groups", "sect"), "tile", "half", None, None),
        P(None, ("groups", "sect"), "tile", "half"),
        P(None, ("groups", "sect"), "tile", "half"),
    )
    out_specs = (
        P(("groups", "sect"), "tile", "half", None, None),
        P(("groups", "sect"), "tile", "half"),
    )
    return jax.shard_map(body, mesh=mesh, in_specs=in_specs, out_specs=out_specs, check_vma=False)
```
